32 devices in a mesh: dp: 8 (over z, y), ctx: 4 (over x, core).
Axes of the slice: x: 2, y: 2, z: 4, core: 2. Of those that a mesh axis runs over, the one named last changes fastest.
Arguments:
- tokens: bfloat16 [8, 512, 2048], P('dp', 'ctx'), may hold values from -6 to 6
- segment_ids: int32 [8, 512], P('dp'), may hold values from 0 to 2, as said below
- gain_first: bfloat16 [2048], P(('dp', 'ctx')), may hold values from 0.5 to 1.5
- qkv_weight: bfloat16 [2048, 6144], P(('dp', 'ctx')), may hold values from -0.125 to 0.125
- out_weight: bfloat16 [2048, 2048], P(('dp', 'ctx')), may hold values from -1 to 1
- gain_second: bfloat16 [2048], P(('dp', 'ctx')), may hold values from 0.5 to 1.5
- gate_up_weight: bfloat16 [2048, 16384], P(('dp', 'ctx')), may hold values from -0.125 to 0.125
- down_weight: bfloat16 [8192, 2048], P(('dp', 'ctx')), may hold values from -0.0625 to 0.0625
- cotangent: bfloat16 [8, 512, 2048], P('dp', 'ctx'), may hold values from -6 to 6
Outputs:
- mixed: bfloat16 [8, 512, 2048], P('dp', 'ctx')
- input_grad: float32 [8, 512, 2048], P('dp', 'ctx')
- gain_first_grad: float32 [2048], P(('dp', 'ctx'))
- qkv_weight_grad: float32 [2048, 6144], P(('dp', 'ctx'))
- out_weight_grad: float32 [2048, 2048], P(('dp', 'ctx'))
- gain_second_grad: float32 [2048], P(('dp', 'ctx'))
- gate_up_weight_grad: float32 [2048, 16384], P(('dp', 'ctx'))
- down_weight_grad: float32 [8192, 2048], P(('dp', 'ctx'))
The draws below stay inside these ranges and needn't reach their ends.
Inputs may be any that keep to these rules, and one draw needn't show every extreme that they name: `segment_ids`: in each sequence the ids never fall and name three documents 0, 1, 2, each of one token or more; document 1 begins within the first 128 positions and ends within the last 128 positions.
All inputs are finite; a program needn't handle non-finite values.
Results may differ from the reference program's by a relative error of at most 0.014.
Values may be sent and summed in bfloat16 or wider, within the bound.
No kernel may reach another device: no remote copies, remote signals or barrier semaphores. Data moves between devices by JAX's collectives and lax.ppermute only.
A program may use at most 512 MiB of HBM per device.

```python
import math
import jax
import jax.numpy as jnp
from jax import lax

D = 2048
HEAD_DIM = 64
FF = 8192
TOK_DEV = 128
SEQ_LEN = 512
SEQS = 8


def draw_segment_ids(key, part):
    key = jax.random.fold_in(key, 11)
    key_start, key_end = jax.random.split(key)
    begins = jax.random.randint(key_start, (SEQS, 1), 1, TOK_DEV)
    endings = jax.random.randint(key_end, (SEQS, 1), SEQ_LEN - TOK_DEV + 1, SEQ_LEN)
    places = jnp.arange(SEQ_LEN)[None, :]
    return (places >= begins).astype(jnp.int32) + (places >= endings).astype(jnp.int32)


def shard_levels(own_key, dims, pieces, low, top_value):
    loudness, own = 1.0, jax.random.fold_in(own_key, 6)
    for position, blocks in pieces:
        heights = jnp.exp(jax.random.uniform(jax.random.fold_in(own, position), (blocks,), jnp.float32, low / len(pieces), top_value / len(pieces)))
        loudness = loudness * jnp.repeat(heights, dims[position] // blocks).reshape([-1 if axis == position else 1 for axis in range(len(dims))])
    return loudness


def scatter_about(own_key, shape, scale, bound, pieces=(), dtype=jnp.bfloat16):
    result = scale * jax.random.normal(own_key, shape, jnp.float32)
    if pieces:
        result = result * shard_levels(own_key, shape, pieces, -0.22, 0.18)
    return jnp.clip(result, -bound, bound).astype(dtype)


def setup_inputs(seed: int = 0) -> dict:
    arg_keys = jax.random.split(jax.random.key(seed), 10)
    tokens = scatter_about(arg_keys[0], (SEQS, SEQ_LEN, D), 1.0, 6.0, ((0, 8), (1, 4)))
    segment_ids = draw_segment_ids(jax.random.fold_in(arg_keys[9], 71), 0)
    gain_first = jnp.clip(1.0 + 0.1 * jax.random.normal(arg_keys[2], (D,), jnp.float32), 0.5, 1.5).astype(jnp.bfloat16)
    qkv_weight = scatter_about(arg_keys[3], (D, 3 * D), D ** -0.5, 0.125, ((0, 32),))
    out_weight = scatter_about(arg_keys[4], (D, D), (D // 64) ** -0.5, 1.0, ((0, 32),))
    gain_second = jnp.clip(1.0 + 0.1 * jax.random.normal(arg_keys[5], (D,), jnp.float32), 0.5, 1.5).astype(jnp.bfloat16)
    gate_up_weight = scatter_about(arg_keys[6], (D, 2 * FF), D ** -0.5, 0.125, ((0, 32),))
    down_weight = scatter_about(arg_keys[7], (FF, D), FF ** -0.5, 0.0625, ((0, 32),))
    cotangent = scatter_about(arg_keys[8], (SEQS, SEQ_LEN, D), 1.0, 6.0, ((0, 8), (1, 4)))
    return dict(tokens=tokens, segment_ids=segment_ids, gain_first=gain_first, qkv_weight=qkv_weight, out_weight=out_weight, gain_second=gain_second, gate_up_weight=gate_up_weight, down_weight=down_weight, cotangent=cotangent)


epsilon = 1e-05
rope_base = 130000.0
highest = lax.Precision.HIGHEST

@jax.custom_vjp
def low(v):
    return lax.optimization_barrier(v.astype(jnp.bfloat16)).astype(jnp.float32)

@jax.custom_vjp
def low_back(v):
    return v

def low_keep(v):
    return (low(v), None)

def low_pass(kept, grad):
    return (grad,)

def back_keep(v):
    return (v, None)

def back_low(kept, grad):
    return (low(grad),)
low.defvjp(low_keep, low_pass)
low_back.defvjp(back_keep, back_low)

def rotation(length):
    half_dim = HEAD_DIM // 2
    places = jnp.arange(length).astype(jnp.float32)
    freqs = jnp.exp(jnp.arange(half_dim).astype(jnp.float32) * (-2.0 * math.log(rope_base) / HEAD_DIM))
    angles = places[:, None] * freqs[None, :]
    return (jnp.cos(angles)[:, None, :], jnp.sin(angles)[:, None, :])

def rotate_pairs(values, cosines, sines):
    half_dim = HEAD_DIM // 2
    lower_half = values[..., :half_dim]
    upper_half = values[..., half_dim:]
    return jnp.concatenate([lower_half * cosines - upper_half * sines, upper_half * cosines + lower_half * sines], -1)

def normalize(values, gain):
    return values * lax.rsqrt(lax.optimization_barrier(jnp.mean(values * values, -1, keepdims=True)) + epsilon) * gain

def attend(queries, key_block, values, segments):
    block_rows = min(512, SEQ_LEN)
    block_count = SEQ_LEN // block_rows
    key_index = jnp.arange(SEQ_LEN).astype(jnp.int32)
    score_scale = HEAD_DIM ** (-0.5)

    @jax.checkpoint
    def one_block(offset):
        query_block = lax.dynamic_slice_in_dim(queries, offset, block_rows, 0)
        query_segments = lax.dynamic_slice_in_dim(segments, offset, block_rows, 0)
        scores = jnp.einsum('qhd,khd->hqk', query_block, key_block, precision=highest) * score_scale
        scores = low_back(scores)
        query_index = offset + jnp.arange(block_rows).astype(jnp.int32)
        allowed = (key_index[None, :] <= query_index[:, None]) & (segments[None, :] == query_segments[:, None])
        scores = jnp.where(allowed[None], scores, -1e+30)
        weights_low = low(jax.nn.softmax(scores, axis=-1))
        return jnp.einsum('hqk,khd->qhd', weights_low, values, precision=highest)
    starts = (jnp.arange(block_count) * block_rows).astype(jnp.int32)
    blocks = lax.map(one_block, starts)
    return blocks.reshape(SEQ_LEN, -1)

def forward_layer(inputs, gain_first, qkv_weight, out_weight, gain_second, gate_up_weight, down_weight, segments):
    group_size, length, model_width = inputs.shape
    head_count = model_width // HEAD_DIM
    cosines, sines = rotation(length)
    normed_one = low(normalize(inputs, gain_first))
    mixed_qkv = low_back(jnp.einsum('gld,de->gle', normed_one, qkv_weight, precision=highest))
    shaped = mixed_qkv.reshape(group_size, length, 3, head_count, HEAD_DIM)
    queries = low(rotate_pairs(shaped[:, :, 0], cosines, sines))
    key_rot = low(rotate_pairs(shaped[:, :, 1], cosines, sines))
    values = low(shaped[:, :, 2])
    attended = lax.map(lambda bundle: attend(*bundle), (queries, key_rot, values, segments))
    attended = low(low_back(attended))
    residual = inputs + low_back(jnp.einsum('gld,de->gle', attended, out_weight, precision=highest))
    normed_two = low(normalize(residual, gain_second))
    gate_up = low_back(jnp.einsum('gld,de->gle', normed_two, gate_up_weight, precision=highest))
    hidden = low(jax.nn.silu(gate_up[..., :FF]) * gate_up[..., FF:])
    return residual + low_back(jnp.einsum('glf,fd->gld', hidden, down_weight, precision=highest))

def reference(tokens, segment_ids, gain_first, qkv_weight, out_weight, gain_second, gate_up_weight, down_weight, cotangent):
    group_size = 4 if SEQS % 4 == 0 else 1
    step_count = SEQS // group_size
    params = tuple((member.astype(jnp.float32) for member in (gain_first, qkv_weight, out_weight, gain_second, gate_up_weight, down_weight)))
    inputs = tokens.astype(jnp.float32).reshape(step_count, group_size, SEQ_LEN, D)
    segments = segment_ids.reshape(step_count, group_size, SEQ_LEN)
    upstream = cotangent.astype(jnp.float32).reshape(step_count, group_size, SEQ_LEN, D)

    def advance(totals, bundle):
        block_inputs, block_segments, block_upstream = bundle

        def forward(block_values, *weights):
            return forward_layer(block_values, *weights, block_segments)
        output, pull = jax.vjp(forward, block_inputs, *params)
        grads = pull(block_upstream)
        totals = tuple((left + right for left, right in zip(totals, grads[1:])))
        return (totals, (output, grads[0]))
    zeros = tuple((jnp.zeros(member.shape, jnp.float32) for member in params))
    totals, (outputs, input_grads) = lax.scan(advance, zeros, (inputs, segments, upstream))
    return (outputs.reshape(SEQS, SEQ_LEN, D).astype(jnp.bfloat16), input_grads.reshape(SEQS, SEQ_LEN, D), totals[0], totals[1], totals[2], totals[3], totals[4], totals[5])
```

```python
import math

import jax
import jax.numpy as jnp
from jax import lax
from jax.sharding import Mesh, PartitionSpec as P

HEAD_DIM = 64
EPSILON = 1e-05
ROPE_BASE = 130000.0
LOW = jnp.bfloat16
FULL = jnp.float32


def shift(value, axis, step):
    size = lax.axis_size(axis)
    if step % size == 0:
        return value
    return lax.ppermute(value, axis, [(i, (i + step) % size) for i in range(size)])


def product(left, right):
    return jnp.dot(left, right, preferred_element_type=FULL)


def product_t(left, right):
    return lax.dot_general(left, right, (((1,), (1,)), ((), ())), preferred_element_type=FULL)


def t_product(left, right):
    return lax.dot_general(left, right, (((0,), (0,)), ((), ())), preferred_element_type=FULL)


def rotation(positions):
    half_dim = HEAD_DIM // 2
    freqs = jnp.exp(
        jnp.arange(half_dim).astype(FULL) * (-2.0 * math.log(ROPE_BASE) / HEAD_DIM)
    )
    angles = positions[:, None] * freqs[None, :]
    return (jnp.cos(angles)[:, None, :], jnp.sin(angles)[:, None, :])


def rotate_pairs(values, cosines, sines):
    row_count = values.shape[0]
    pieces = values.reshape(row_count, -1, HEAD_DIM)
    half_dim = HEAD_DIM // 2
    lower_half = pieces[..., :half_dim]
    upper_half = pieces[..., half_dim:]
    turned = jnp.concatenate(
        [lower_half * cosines - upper_half * sines, upper_half * cosines + lower_half * sines], -1
    )
    return turned.reshape(row_count, -1)


def gather_sequence(block, step):
    own = shift(block, "a", step)
    pieces = [shift(own, "x", jx) for jx in range(lax.axis_size("x"))]
    return [shift(piece, "c", jc) for jc in range(lax.axis_size("c")) for piece in pieces]


def gather_tokens(block):
    return [
        jnp.concatenate(gather_sequence(block, step), 0) for step in range(lax.axis_size("a"))
    ]


def scatter_tokens(parts, rows):
    x_size, c_size = lax.axis_size("x"), lax.axis_size("c")
    total = None
    order = list(range(1, len(parts))) + [0]
    for step in order:
        grid = parts[step].reshape(c_size, x_size, rows, -1)
        here = grid[0]
        for jc in range(1, c_size):
            here = here + shift(grid[jc].astype(LOW), "c", -jc).astype(FULL)
        own = here[0]
        for jx in range(1, x_size):
            own = own + shift(here[jx].astype(LOW), "x", -jx).astype(FULL)
        if step:
            own = shift(own.astype(LOW), "a", -step).astype(FULL)
        total = own if total is None else total + own
    return total


GROUP = ("a", "x", "c")
EVERY = ("a", "w", "x", "c")


def swap_blocks(blocks):
    return lax.all_to_all(blocks, GROUP, 0, 0, tiled=True)


def gather_w(block):
    size, rank = lax.axis_size("w"), lax.axis_index("w")
    whole = jnp.zeros((size,) + block.shape, block.dtype)
    for step in range(size):
        whole = lax.dynamic_update_index_in_dim(
            whole, shift(block, "w", step), (rank - step) % size, 0
        )
    return whole


def scatter_w(blocks, axis):
    size, rank = lax.axis_size("w"), lax.axis_index("w")
    total = lax.dynamic_index_in_dim(blocks, rank, axis, keepdims=False)
    for step in range(1, size):
        sent = lax.dynamic_index_in_dim(blocks, (rank - step) % size, axis, keepdims=False)
        total = total + shift(sent.astype(LOW), "w", -step).astype(FULL)
    return total


def shards(
    tokens,
    segment_ids,
    gain_first,
    qkv_weight,
    out_weight,
    gain_second,
    gate_up_weight,
    down_weight,
    cotangent,
):
    a_size, w_size = lax.axis_size("a"), lax.axis_size("w")
    x_size, c_size = lax.axis_size("x"), lax.axis_size("c")
    ctx_size = x_size * c_size
    group = a_size * ctx_size
    x_rank, c_rank = lax.axis_index("x"), lax.axis_index("c")
    own_tokens = tokens[0]
    rows, width = own_tokens.shape
    weight_rows = qkv_weight.shape[0]
    units = down_weight.shape[0]
    head_cols = width // group
    heads = head_cols // HEAD_DIM
    score_scale = HEAD_DIM ** (-0.5)

    gain_one = gain_first.astype(FULL)[:, None]
    gain_two = gain_second.astype(FULL)[:, None]
    qkv_scaled = (qkv_weight.astype(FULL) * gain_one).astype(LOW)
    qkv_blocks = qkv_scaled.reshape(weight_rows, 3, group, head_cols).transpose(2, 0, 1, 3)
    qkv_blocks = swap_blocks(qkv_blocks.reshape(group, weight_rows, 3 * head_cols))

    def ordered_rows(blocks):
        whole = gather_w(blocks)
        columns = blocks.shape[-1]
        whole = whole.reshape(w_size, a_size, ctx_size, weight_rows, columns)
        return whole.transpose(1, 0, 2, 3, 4).reshape(width, columns)

    qkv_cols = ordered_rows(qkv_blocks)
    gate_up_scaled = (gate_up_weight.astype(FULL) * gain_two).astype(LOW)
    gate_up_blocks = gate_up_scaled.reshape(
        weight_rows, 2, a_size, w_size, ctx_size, units
    ).transpose(2, 4, 0, 1, 3, 5)
    own_units = w_size * units
    gate_up_blocks = swap_blocks(gate_up_blocks.reshape(group, weight_rows, 2 * own_units))
    gate_up_cols = ordered_rows(gate_up_blocks)
    down_rows = gather_w(down_weight).reshape(own_units, width)
    out_full = lax.all_gather(out_weight, EVERY, axis=0, tiled=True)

    places = [
        ((x_rank - jx) % x_size) * c_size + (c_rank - jc) % c_size
        for jc in range(c_size)
        for jx in range(x_size)
    ]
    positions = jnp.concatenate(
        [place * rows + jnp.arange(rows, dtype=jnp.int32) for place in places]
    )
    cosines, sines = rotation(positions.astype(FULL))
    own_segments = jnp.concatenate(
        [lax.dynamic_slice_in_dim(segment_ids[0], place * rows, rows) for place in places]
    )
    segments = [shift(own_segments, "a", step) for step in range(a_size)]
    causal = positions[None, :] <= positions[:, None]

    def norm_scale(values):
        return lax.rsqrt(jnp.mean(values * values, -1, keepdims=True) + EPSILON)

    token_blocks = gather_tokens(own_tokens)
    branch_grads = gather_tokens(cotangent[0])

    def split_heads(values):
        return values.reshape(values.shape[0], heads, HEAD_DIM)

    scaled_ones, queries, keys, values, probs_all, attended_blocks = [], [], [], [], [], []
    for step in range(a_size):
        block = token_blocks[step].astype(FULL)
        scaled = (block * norm_scale(block)).astype(LOW)
        mixed_qkv = product(scaled, qkv_cols)
        query = split_heads(rotate_pairs(mixed_qkv[:, :head_cols], cosines, sines).astype(LOW))
        key = split_heads(
            rotate_pairs(mixed_qkv[:, head_cols : 2 * head_cols], cosines, sines).astype(LOW)
        )
        value = split_heads(mixed_qkv[:, 2 * head_cols :].astype(LOW))
        allowed = causal & (segments[step][None, :] == segments[step][:, None])
        scores = jnp.einsum("qhd,khd->hqk", query, key, preferred_element_type=FULL) * score_scale
        scores = jnp.where(allowed[None], scores, -1e30)
        expanded = jnp.exp(scores - jnp.max(scores, -1, keepdims=True))
        probs = expanded / jnp.sum(expanded, -1, keepdims=True)
        attended = jnp.einsum("hqk,khd->qhd", probs.astype(LOW), value, preferred_element_type=FULL)
        scaled_ones.append(scaled)
        queries.append(query)
        keys.append(key)
        values.append(value)
        probs_all.append(probs)
        attended_blocks.append(attended.reshape(-1, head_cols).astype(LOW))

    def to_owners(blocks):
        a_rank = lax.axis_index("a")
        whole = jnp.zeros((a_size, ctx_size, rows, head_cols), LOW)
        for step in range(a_size):
            pieces = blocks[step].reshape(ctx_size, rows, head_cols)
            for index, place in enumerate(places):
                whole = lax.dynamic_update_slice(
                    whole, pieces[index][None, None], ((a_rank - step) % a_size, place, 0, 0)
                )
        swapped = swap_blocks(whole.reshape(group, rows, head_cols))
        return swapped.transpose(1, 0, 2).reshape(rows, width)

    def to_heads(block):
        a_rank = lax.axis_index("a")
        swapped = swap_blocks(block.reshape(rows, group, head_cols).transpose(1, 0, 2))
        whole = swapped.reshape(a_size, ctx_size, rows, head_cols)
        return [
            jnp.concatenate(
                [
                    lax.dynamic_slice(
                        whole, ((a_rank - step) % a_size, place, 0, 0), (1, 1, rows, head_cols)
                    )[0, 0]
                    for place in places
                ],
                0,
            )
            for step in range(a_size)
        ]

    attended_own = to_owners(attended_blocks)
    inputs = own_tokens.astype(FULL)
    residual = inputs + product(attended_own, out_full)
    inverse_two = norm_scale(residual)
    scaled_two = residual * inverse_two
    scaled_twos = gather_tokens(scaled_two.astype(LOW))

    hiddens, gate_up_grads, mixed_parts, two_parts = [], [], [], []
    for step in range(a_size):
        gate_up = product(scaled_twos[step], gate_up_cols)
        gate = gate_up[:, :own_units]
        upper = gate_up[:, own_units:]
        sigmoid = jax.nn.sigmoid(gate)
        hidden = (gate * sigmoid * upper).astype(LOW)
        hidden_grad = product_t(branch_grads[step], down_rows)
        gate_grad = hidden_grad * upper * sigmoid * (1.0 + gate * (1.0 - sigmoid))
        upper_grad = hidden_grad * (gate * sigmoid)
        gate_up_grad_low = jnp.concatenate([gate_grad, upper_grad], 1).astype(LOW)
        two_parts.append(product_t(gate_up_grad_low, gate_up_cols))
        mixed_parts.append(product(hidden, down_rows))
        hiddens.append(hidden)
        gate_up_grads.append(gate_up_grad_low)

    weighted_two = scatter_tokens(two_parts, rows)
    upstream = cotangent[0].astype(FULL)
    residual_grad = upstream + inverse_two * (
        weighted_two - scaled_two * jnp.mean(weighted_two * scaled_two, -1, keepdims=True)
    )
    attn_grad_low = residual_grad.astype(LOW)
    attended_grads = to_heads(product_t(attn_grad_low, out_full).astype(LOW))

    down_term = t_product(jnp.concatenate(hiddens, 0), jnp.concatenate(branch_grads, 0))
    down_grad = scatter_w(down_term.reshape(w_size, units, width), 0)
    gate_up_term = t_product(jnp.concatenate(scaled_twos, 0), jnp.concatenate(gate_up_grads, 0))

    def to_row_owners(term):
        columns = term.shape[-1]
        mine = scatter_w(term.reshape(a_size, w_size, ctx_size, weight_rows, columns), 1)
        return swap_blocks(mine.astype(LOW).reshape(group, weight_rows, columns)).astype(FULL)

    gate_up_rows = to_row_owners(gate_up_term)
    gate_up_raw = (
        gate_up_rows.reshape(a_size, ctx_size, weight_rows, 2, w_size, units)
        .transpose(2, 3, 0, 4, 1, 5)
        .reshape(weight_rows, -1)
    )
    gate_up_grad = gate_up_raw * gain_two
    gain_two_grad = jnp.sum(gate_up_raw * gate_up_weight.astype(FULL), 1)
    mixed = (residual + scatter_tokens(mixed_parts, rows)).astype(LOW)
    out_grad = lax.psum_scatter(
        t_product(attended_own, attn_grad_low).astype(LOW), EVERY, scatter_dimension=0, tiled=True
    ).astype(FULL)

    one_parts, qkv_grads = [], []
    for step in range(a_size):
        grad = split_heads(attended_grads[step])
        probs = probs_all[step]
        value_grad = jnp.einsum("hqk,qhd->khd", probs.astype(LOW), grad, preferred_element_type=FULL)
        prob_grad = jnp.einsum("qhd,khd->hqk", grad, values[step], preferred_element_type=FULL)
        row_terms = jnp.sum(probs * prob_grad, -1, keepdims=True)
        score_grad = (probs * (prob_grad - row_terms)).astype(LOW)
        query_grad = score_scale * jnp.einsum(
            "hqk,khd->qhd", score_grad, keys[step], preferred_element_type=FULL
        )
        key_grad = score_scale * jnp.einsum(
            "hqk,qhd->khd", score_grad, queries[step], preferred_element_type=FULL
        )
        qkv_grad_low = jnp.concatenate(
            [
                rotate_pairs(query_grad.reshape(-1, head_cols), cosines, -sines),
                rotate_pairs(key_grad.reshape(-1, head_cols), cosines, -sines),
                value_grad.reshape(-1, head_cols),
            ],
            1,
        ).astype(LOW)
        qkv_grads.append(qkv_grad_low)
        one_parts.append(product_t(qkv_grad_low, qkv_cols))

    weighted_one = scatter_tokens(one_parts, rows)
    inverse_one = norm_scale(inputs)
    scaled_one = inputs * inverse_one
    input_grad = residual_grad + inverse_one * (
        weighted_one - scaled_one * jnp.mean(weighted_one * scaled_one, -1, keepdims=True)
    )
    qkv_term = t_product(jnp.concatenate(scaled_ones, 0), jnp.concatenate(qkv_grads, 0))
    qkv_raw = (
        to_row_owners(qkv_term)
        .reshape(group, weight_rows, 3, head_cols)
        .transpose(1, 2, 0, 3)
        .reshape(weight_rows, -1)
    )
    qkv_grad = qkv_raw * gain_one
    gain_one_grad = jnp.sum(qkv_raw * qkv_weight.astype(FULL), 1)
    return (
        mixed[None],
        input_grad[None],
        gain_one_grad,
        qkv_grad,
        out_grad,
        gain_two_grad,
        gate_up_grad,
        down_grad,
    )


def solution(mesh):
    dp_size, ctx_size = mesh.devices.shape
    a_size = math.gcd(dp_size, 4)
    fine = Mesh(
        mesh.devices.reshape(a_size, dp_size // a_size, ctx_size // 2, 2), ("a", "w", "x", "c")
    )
    flat = ("a", "w", "x", "c")
    token_spec = P(("a", "w"), ("x", "c"), None)
    return jax.shard_map(
        shards,
        mesh=fine,
        in_specs=(
            token_spec,
            P(("a", "w"), None),
            P(flat),
            P(flat, None),
            P(flat, None),
            P(flat),
            P(flat, None),
            P(flat, None),
            token_spec,
        ),
        out_specs=(
            token_spec,
            token_spec,
            P(flat),
            P(flat, None),
            P(flat, None),
            P(flat),
            P(flat, None),
            P(flat, None),
        ),
        check_vma=False,
    )
```

```python
import functools
import math

import jax
import jax.numpy as jnp
from jax import lax
from jax.experimental import pallas as pl
from jax.experimental.pallas import tpu as pltpu
from jax.sharding import Mesh, PartitionSpec as P

HEAD_DIM = 64
EPSILON = 1e-05
ROPE_BASE = 130000.0
LANES = 128
LOW = jnp.bfloat16
FULL = jnp.float32
VMEM_BYTES = 50 * 1024 * 1024

CUBE = ("p", "q", "x")
GROUP = ("p", "q", "x", "c")
EVERY = ("w", "p", "q", "x", "c")


def shift(value, axis, step):
    size = lax.axis_size(axis)
    if step % size == 0:
        return value
    return lax.ppermute(value, axis, [(i, (i + step) % size) for i in range(size)])


def flip(value, axis):
    return shift(value, axis, 1)


def after(value, *earlier):
    return lax.optimization_barrier((value,) + earlier)[0]


def product(left, right):
    return jnp.dot(left, right, preferred_element_type=FULL)


def product_t(left, right):
    return lax.dot_general(left, right, (((1,), (1,)), ((), ())), preferred_element_type=FULL)


def t_product(left, right):
    return lax.dot_general(left, right, (((0,), (0,)), ((), ())), preferred_element_type=FULL)


def gather_tokens(block, last="x"):
    first, second = [axis for axis in CUBE if axis != last][:2]
    one = flip(block, first)
    two = flip(block, second)
    three = flip(block, last)
    one_two = flip(one, second)
    two_three = flip(two, last)
    three_one = flip(three, first)
    corner = flip(one_two, last)
    held = {
        frozenset(): block,
        frozenset((first,)): one,
        frozenset((second,)): two,
        frozenset((last,)): three,
        frozenset((first, second)): one_two,
        frozenset((second, last)): two_three,
        frozenset((last, first)): three_one,
        frozenset(CUBE): corner,
    }
    sequences = []
    for place in ((), ("p",), ("q",), ("p", "q")):
        pair = jnp.concatenate([held[frozenset(place)], held[frozenset(place + ("x",))]], 0)
        sequences.append(jnp.concatenate([pair, flip(pair, "c")], 0))
    return sequences


def scatter_tokens(parts, rows, last="x"):
    first, second = [axis for axis in CUBE if axis != last][:2]
    held = {}
    for place, part in reversed(list(zip(((), ("p",), ("q",), ("p", "q")), parts))):
        grid = part.reshape(2, 2 * rows, -1)
        pair = grid[0].astype(FULL) + flip(grid[1].astype(LOW), "c").astype(FULL)
        held[frozenset(place)] = pair[:rows]
        held[frozenset(place + ("x",))] = pair[rows:]

    def send(key, axis):
        value = held[frozenset(key)].astype(LOW)
        return flip(value, axis).astype(FULL)

    def add(key, *terms):
        for term in terms:
            held[frozenset(key)] = held[frozenset(key)] + term

    add((first, second), send(CUBE, last))
    one, two, three = (
        send((first, second), second),
        send((second, last), last),
        send((last, first), first),
    )
    add((first,), one)
    add((second,), two)
    add((last,), three)
    add((), send((first,), first), send((second,), second), send((last,), last))
    return held[frozenset()]


def swap_blocks(blocks):
    return lax.all_to_all(blocks, GROUP, 0, 0, tiled=True)


def spread_kernel(places, chunk, weight_ref, gain_ref, out_ref):
    gain = gain_ref[...]
    for place in range(places):
        piece = weight_ref[:, place * chunk : (place + 1) * chunk].astype(FULL) * gain
        out_ref[place] = piece.astype(LOW)


def spread(weight, gain, places, chunk):
    rows, columns = weight.shape
    count = columns // (places * chunk)
    if chunk % LANES:
        scaled = (weight.astype(FULL) * gain).astype(LOW)
        blocks = scaled.reshape(rows, count, places, chunk).transpose(2, 0, 1, 3)
        return blocks.reshape(places, rows, count * chunk)
    return pl.pallas_call(
        functools.partial(spread_kernel, places, chunk),
        grid=(count,),
        in_specs=[
            pl.BlockSpec((rows, places * chunk), lambda i: (0, i)),
            pl.BlockSpec((rows, 1), lambda i: (0, 0)),
        ],
        out_specs=pl.BlockSpec((places, rows, chunk), lambda i: (0, 0, i)),
        out_shape=jax.ShapeDtypeStruct((places, rows, count * chunk), LOW),
        compiler_params=pltpu.CompilerParams(vmem_limit_bytes=VMEM_BYTES),
    )(weight, gain)


def collect_kernel(places, chunk, blocks_ref, weight_ref, gain_ref, grad_ref, total_ref):
    gain = gain_ref[...]

    @pl.when(pl.program_id(0) == 0)
    def _():
        total_ref[...] = jnp.zeros_like(total_ref)

    total = total_ref[...]
    for place in range(places):
        piece = blocks_ref[place].astype(FULL)
        grad_ref[:, place * chunk : (place + 1) * chunk] = piece * gain
        terms = piece * weight_ref[:, place * chunk : (place + 1) * chunk].astype(FULL)
        for start in range(0, chunk, LANES):
            total = total + terms[:, start : start + LANES]
    total_ref[...] = total


def collect(blocks, weight, gain, chunk):
    places, rows, _ = blocks.shape
    columns = weight.shape[1]
    count = columns // (places * chunk)
    if chunk % LANES:
        raw = blocks.reshape(places, rows, count, chunk).transpose(1, 2, 0, 3)
        raw = raw.reshape(rows, columns).astype(FULL)
        return raw * gain, jnp.sum(raw * weight.astype(FULL), 1)
    grad, total = pl.pallas_call(
        functools.partial(collect_kernel, places, chunk),
        grid=(count,),
        in_specs=[
            pl.BlockSpec((places, rows, chunk), lambda i: (0, 0, i)),
            pl.BlockSpec((rows, places * chunk), lambda i: (0, i)),
            pl.BlockSpec((rows, 1), lambda i: (0, 0)),
        ],
        out_specs=[
            pl.BlockSpec((rows, places * chunk), lambda i: (0, i)),
            pl.BlockSpec((rows, LANES), lambda i: (0, 0)),
        ],
        out_shape=[
            jax.ShapeDtypeStruct((rows, columns), FULL),
            jax.ShapeDtypeStruct((rows, LANES), FULL),
        ],
        compiler_params=pltpu.CompilerParams(vmem_limit_bytes=VMEM_BYTES),
    )(blocks, weight, gain)
    return grad, jnp.sum(total, 1)


def gather_w(block):
    size, rank = lax.axis_size("w"), lax.axis_index("w")
    whole = jnp.zeros((size,) + block.shape, block.dtype)
    for step in range(size):
        whole = lax.dynamic_update_index_in_dim(
            whole, shift(block, "w", step), (rank - step) % size, 0
        )
    return whole.reshape((size * block.shape[0],) + block.shape[1:])


def weight_grad(left, right):
    size, rank = lax.axis_size("w"), lax.axis_index("w")
    rows = left.shape[1] // size

    def term(place):
        return t_product(lax.dynamic_slice_in_dim(left, place * rows, rows, 1), right)

    received = [
        shift(term((rank - step) % size).astype(LOW), "w", -step) for step in range(1, size)
    ]
    total = term(rank)
    for piece in received:
        total = total + piece.astype(FULL)
    return total


def rotate(values, cosines, sines, lower):
    half_dim = HEAD_DIM // 2
    width = values.shape[-1]
    other = jnp.where(
        lower, pltpu.roll(values, width - half_dim, 1), pltpu.roll(values, half_dim, 1)
    )
    return values * cosines + other * sines


def lower_half(shape):
    return lax.broadcasted_iota(jnp.int32, shape, 1) % HEAD_DIM < HEAD_DIM // 2


def head_lanes(shape, head):
    return lax.broadcasted_iota(jnp.int32, shape, 1) // HEAD_DIM == head


def attend_kernel(
    heads, tokens_ref, weight_ref, cos_ref, sin_ref, pos_col, pos_row, seg_col, seg_row,
    scaled_ref, qkv_ref, log_ref, out_ref,
):
    cols = heads * HEAD_DIM
    block = tokens_ref[...].astype(FULL)
    mean = jnp.mean(block * block, -1, keepdims=True)
    scaled = (block * lax.rsqrt(mean + EPSILON)).astype(LOW)
    scaled_ref[...] = scaled
    mixed = product(scaled, weight_ref[...])
    cosines, sines = cos_ref[...], sin_ref[...]
    lower = lower_half(cosines.shape)
    query = rotate(mixed[:, :cols], cosines, sines, lower).astype(LOW)
    key = rotate(mixed[:, cols : 2 * cols], cosines, sines, lower).astype(LOW)
    value = mixed[:, 2 * cols :].astype(LOW)
    qkv_ref[:, :cols] = query
    qkv_ref[:, cols : 2 * cols] = key
    qkv_ref[:, 2 * cols :] = value
    allowed = (pos_row[...] <= pos_col[...]) & (seg_row[...] == seg_col[...])
    logs = jnp.zeros(query.shape, FULL)
    attended = jnp.zeros(query.shape, FULL)
    for head in range(heads):
        own = head_lanes(query.shape, head)
        scores = product_t(jnp.where(own, query, 0), key) * HEAD_DIM**-0.5
        scores = jnp.where(allowed, scores, -1e30)
        highest = jnp.max(scores, -1, keepdims=True)
        expanded = jnp.exp(scores - highest)
        denominator = jnp.sum(expanded, -1, keepdims=True)
        probs_low = (expanded / denominator).astype(LOW)
        attended = jnp.where(own, product(probs_low, value), attended)
        logs = jnp.where(own, highest + jnp.log(denominator), logs)
    log_ref[...] = logs
    out_ref[...] = attended.astype(LOW)


def attend_back_kernel(
    heads, qkv_ref, log_ref, grad_ref, weight_ref, cos_ref, sin_ref, pos_col, pos_row,
    seg_col, seg_row, qkv_grad_ref, part_ref,
):
    cols = heads * HEAD_DIM
    query = qkv_ref[:, :cols]
    key = qkv_ref[:, cols : 2 * cols]
    value = qkv_ref[:, 2 * cols :]
    grad = grad_ref[...]
    allowed = (pos_row[...] <= pos_col[...]) & (seg_row[...] == seg_col[...])
    query_grad = jnp.zeros(query.shape, FULL)
    key_grad = jnp.zeros(query.shape, FULL)
    value_grad = jnp.zeros(query.shape, FULL)
    score_scale = HEAD_DIM**-0.5
    for head in range(heads):
        own = head_lanes(query.shape, head)
        scores = product_t(jnp.where(own, query, 0), key) * score_scale
        log_total = log_ref[:, head * HEAD_DIM : head * HEAD_DIM + 1]
        probs = jnp.where(allowed, jnp.exp(jnp.where(allowed, scores - log_total, 0.0)), 0.0)
        value_grad = jnp.where(own, t_product(probs.astype(LOW), grad), value_grad)
        prob_grad = product_t(jnp.where(own, grad, 0), value)
        row_terms = jnp.sum(probs * prob_grad, -1, keepdims=True)
        score_grad = (probs * (prob_grad - row_terms)).astype(LOW)
        query_grad = jnp.where(own, product(score_grad, key), query_grad)
        key_grad = jnp.where(own, t_product(score_grad, query), key_grad)
    cosines, sines = cos_ref[...], sin_ref[...]
    lower = lower_half(cosines.shape)
    query_low = rotate(query_grad * score_scale, cosines, -sines, lower).astype(LOW)
    key_low = rotate(key_grad * score_scale, cosines, -sines, lower).astype(LOW)
    value_low = value_grad.astype(LOW)
    qkv_grad_ref[:, :cols] = query_low
    qkv_grad_ref[:, cols : 2 * cols] = key_low
    qkv_grad_ref[:, 2 * cols :] = value_low
    weight = weight_ref
    part = product_t(query_low, weight[:, :cols])
    part = part + product_t(key_low, weight[:, cols : 2 * cols])
    part = part + product_t(value_low, weight[:, 2 * cols :])
    part_ref[...] = part.astype(LOW)


def shards(
    tokens,
    segment_ids,
    gain_first,
    qkv_weight,
    out_weight,
    gain_second,
    gate_up_weight,
    down_weight,
    cotangent,
):
    w_size = lax.axis_size("w")
    group = 16
    p_rank, q_rank, x_rank, c_rank = (lax.axis_index(axis) for axis in GROUP)
    own_tokens = tokens[0]
    rows, width = own_tokens.shape
    length = 4 * rows
    units = down_weight.shape[0]
    own_units = w_size * units
    cols = width // group
    heads = cols // HEAD_DIM

    places = [(x_rank ^ jx) * 2 + (c_rank ^ jc) for jc in range(2) for jx in range(2)]
    positions = jnp.concatenate(
        [place * rows + jnp.arange(rows, dtype=jnp.int32) for place in places]
    )
    own_segments = jnp.concatenate(
        [lax.dynamic_slice_in_dim(segment_ids[0], place * rows, rows) for place in places]
    )
    seg_p, seg_q = flip(own_segments, "p"), flip(own_segments, "q")
    segments = [own_segments, seg_p, seg_q, flip(seg_p, "q")]
    half_dim = HEAD_DIM // 2
    freqs = jnp.exp(jnp.arange(half_dim).astype(FULL) * (-2.0 * math.log(ROPE_BASE) / HEAD_DIM))
    angles = positions.astype(FULL)[:, None] * freqs[None, :]
    cosines = jnp.tile(jnp.cos(angles), (1, 2 * heads))
    sines = jnp.tile(jnp.concatenate([-jnp.sin(angles), jnp.sin(angles)], 1), (1, heads))
    pos_col, pos_row = positions[:, None], positions[None, :]

    gain_one = gain_first.astype(FULL)[:, None]
    gain_two = gain_second.astype(FULL)[:, None]
    token_blocks = gather_tokens(own_tokens)
    qkv_cols = gather_w(
        swap_blocks(spread(qkv_weight, gain_one, group, cols)).reshape(-1, 3 * cols)
    )
    down_rows = gather_w(down_weight)
    gate_up_cols = gather_w(
        swap_blocks(spread(gate_up_weight, gain_two, group, units)).reshape(-1, 2 * own_units)
    )
    out_full = lax.all_gather(out_weight, EVERY, axis=0, tiled=True)
    branch_grads = gather_tokens(after(cotangent[0], token_blocks[3]), "q")

    shape = jax.ShapeDtypeStruct
    params = pltpu.CompilerParams(vmem_limit_bytes=VMEM_BYTES)
    attend = pl.pallas_call(
        functools.partial(attend_kernel, heads),
        out_shape=[
            shape((length, width), LOW),
            shape((length, 3 * cols), LOW),
            shape((length, cols), FULL),
            shape((length, cols), LOW),
        ],
        compiler_params=params,
        cost_estimate=pl.CostEstimate(
            flops=2 * length * width * 3 * cols + 4 * heads * length * length * LANES,
            bytes_accessed=4 * length * width + 6 * width * cols,
            transcendentals=heads * length * length,
        ),
    )
    attend_back = pl.pallas_call(
        functools.partial(attend_back_kernel, heads),
        out_shape=[shape((length, 3 * cols), LOW), shape((length, width), LOW)],
        compiler_params=params,
        cost_estimate=pl.CostEstimate(
            flops=2 * length * width * 3 * cols + 10 * heads * length * length * LANES,
            bytes_accessed=2 * length * width + 6 * width * cols,
            transcendentals=heads * length * length,
        ),
    )

    scaled_ones, qkv_lows, logs, attended_blocks = [], [], [], []
    for index in range(4):
        segment = segments[index]
        scaled, qkv_low, log_total, attended = attend(
            token_blocks[index], qkv_cols, cosines, sines, pos_col, pos_row,
            segment[:, None], segment[None, :],
        )
        scaled_ones.append(scaled)
        qkv_lows.append(qkv_low)
        logs.append(log_total)
        attended_blocks.append(attended)

    sequence_places = [
        (p_rank ^ jp) * 2 + (q_rank ^ jq) for jp, jq in ((0, 0), (1, 0), (0, 1), (1, 1))
    ]

    def to_owners(blocks):
        whole = jnp.zeros((4, 4, rows, cols), LOW)
        for sequence, block in zip(sequence_places, blocks):
            for index, place in enumerate(places):
                piece = block[index * rows : (index + 1) * rows]
                whole = lax.dynamic_update_slice(whole, piece[None, None], (sequence, place, 0, 0))
        swapped = swap_blocks(whole.reshape(group, rows, cols))
        return swapped.transpose(1, 0, 2).reshape(rows, width)

    def to_heads(block):
        swapped = swap_blocks(block.reshape(rows, group, cols).transpose(1, 0, 2))
        whole = swapped.reshape(4, 4, rows, cols)
        return [
            jnp.concatenate(
                [
                    lax.dynamic_slice(whole, (sequence, place, 0, 0), (1, 1, rows, cols))[0, 0]
                    for place in places
                ],
                0,
            )
            for sequence in sequence_places
        ]

    def norm_scale(values):
        return lax.rsqrt(jnp.mean(values * values, -1, keepdims=True) + EPSILON)

    attended_own = to_owners(attended_blocks)
    inputs = own_tokens.astype(FULL)
    residual = inputs + product(attended_own, out_full)
    inverse_two = norm_scale(residual)
    scaled_two = residual * inverse_two
    scaled_twos = gather_tokens(scaled_two.astype(LOW))

    hiddens, gate_up_grads, mixed_parts, two_parts = [], [], [], []
    for index in range(4):
        gate_up = product(scaled_twos[index], gate_up_cols)
        gate = gate_up[:, :own_units]
        upper = gate_up[:, own_units:]
        sigmoid = jax.nn.sigmoid(gate)
        hidden = (gate * sigmoid * upper).astype(LOW)
        hidden_grad = product_t(branch_grads[index], down_rows)
        gate_grad = hidden_grad * upper * sigmoid * (1.0 + gate * (1.0 - sigmoid))
        upper_grad = hidden_grad * (gate * sigmoid)
        gate_up_grad_low = jnp.concatenate([gate_grad, upper_grad], 1).astype(LOW)
        two_parts.append(product_t(gate_up_grad_low, gate_up_cols).astype(LOW))
        hiddens.append(hidden)
        gate_up_grads.append(gate_up_grad_low)

    weighted_two = scatter_tokens(two_parts, rows)
    upstream = cotangent[0].astype(FULL)
    residual_grad = upstream + inverse_two * (
        weighted_two - scaled_two * jnp.mean(weighted_two * scaled_two, -1, keepdims=True)
    )
    attn_grad_low = residual_grad.astype(LOW)
    attended_grads = to_heads(product_t(attn_grad_low, out_full).astype(LOW))

    down_grad = weight_grad(jnp.concatenate(hiddens, 0), jnp.concatenate(branch_grads, 0))

    def to_row_owners(mine):
        blocks = mine.astype(LOW).reshape(group, -1, mine.shape[-1])
        return swap_blocks(blocks)

    gate_up_mine = weight_grad(
        jnp.concatenate(scaled_twos, 0), jnp.concatenate(gate_up_grads, 0)
    )
    gate_up_grad, gain_two_grad = collect(
        to_row_owners(gate_up_mine), gate_up_weight, gain_two, units
    )
    mixed_parts = [
        product(after(hidden, weighted_two), down_rows).astype(LOW) for hidden in hiddens
    ]
    mixed = (residual + scatter_tokens(mixed_parts, rows, "q")).astype(LOW)
    out_grad = lax.psum_scatter(
        t_product(attended_own, attn_grad_low).astype(LOW), EVERY, scatter_dimension=0, tiled=True
    ).astype(FULL)

    one_parts, qkv_grads = [None] * 4, [None] * 4
    for index in reversed(range(4)):
        segment = segments[index]
        qkv_grads[index], one_parts[index] = attend_back(
            qkv_lows[index], logs[index], attended_grads[index], qkv_cols, cosines, sines,
            pos_col, pos_row, segment[:, None], segment[None, :],
        )

    qkv_mine = weight_grad(jnp.concatenate(scaled_ones, 0), jnp.concatenate(qkv_grads, 0))
    qkv_grad, gain_one_grad = collect(to_row_owners(qkv_mine), qkv_weight, gain_one, cols)
    weighted_one = scatter_tokens(one_parts, rows)
    inverse_one = norm_scale(inputs)
    scaled_one = inputs * inverse_one
    input_grad = residual_grad + inverse_one * (
        weighted_one - scaled_one * jnp.mean(weighted_one * scaled_one, -1, keepdims=True)
    )
    return (
        mixed[None],
        input_grad[None],
        gain_one_grad,
        qkv_grad,
        out_grad,
        gain_two_grad,
        gate_up_grad,
        down_grad,
    )


def solution(mesh):
    dp_size, _ = mesh.devices.shape
    fine = Mesh(mesh.devices.reshape(dp_size // 4, 2, 2, 2, 2), EVERY)
    token_spec = P(("w", "p", "q"), ("x", "c"), None)
    matrix, vector = P(EVERY, None), P(EVERY)
    return jax.shard_map(
        shards,
        mesh=fine,
        in_specs=(
            token_spec,
            P(("w", "p", "q"), None),
            vector,
            matrix,
            matrix,
            vector,
            matrix,
            matrix,
            token_spec,
        ),
        out_specs=(token_spec, token_spec, vector, matrix, matrix, vector, matrix, matrix),
        check_vma=False,
    )
```

```python
import functools
import math

import jax
import jax.numpy as jnp
from jax import lax
from jax.experimental import pallas as pl
from jax.experimental.pallas import tpu as pltpu
from jax.sharding import Mesh, PartitionSpec as P

HEAD_DIM = 64
EPSILON = 1e-05
ROPE_BASE = 130000.0
LANES = 128
LOW = jnp.bfloat16
FULL = jnp.float32
VMEM_BYTES = 50 * 1024 * 1024

CHUNK = 256

CUBE = ("p", "q", "x")
GROUP = ("p", "q", "x", "c")
PLANE = ("q", "x", "c")
ACROSS = ("w", "p")
EVERY = ("w", "p", "q", "x", "c")


def shift(value, axis, step):
    size = lax.axis_size(axis)
    if step % size == 0:
        return value
    return lax.ppermute(value, axis, [(i, (i + step) % size) for i in range(size)])


def flip(value, axis):
    return shift(value, axis, 1)


def together(*values):
    return lax.optimization_barrier(values)


def after(value, *earlier):
    return lax.optimization_barrier((value,) + earlier)[0]


def product(left, right):
    return jnp.dot(left, right, preferred_element_type=FULL)


def product_t(left, right):
    return lax.dot_general(left, right, (((1,), (1,)), ((), ())), preferred_element_type=FULL)


def t_product(left, right):
    return lax.dot_general(left, right, (((0,), (0,)), ((), ())), preferred_element_type=FULL)


SEQUENCES = ((), ("p",), ("q",), ("p", "q"))


def step(moves, flips, beside=()):
    values = together(*flips, *beside)
    try:
        later = moves.send(values[: len(flips)])
    except StopIteration as end:
        later = end.value
    return later, values[len(flips) :]


def pairs_of(parts, sequences):
    rows = parts[0].shape[0] // len(sequences)
    held = {}
    for index, along_x in enumerate(((), ("x",))):
        other = flip(parts[2 + index], "c")
        for row, place in enumerate(sequences):
            own = slice(row * rows, (row + 1) * rows)
            held[frozenset(place + along_x)] = parts[index][own].astype(FULL) + other[own].astype(
                FULL
            )
    return held


def scatter_steps(parts):
    held = pairs_of(parts, SEQUENCES)

    def send(key, axis):
        return flip(held[frozenset(key)].astype(LOW), axis)

    def add(key, *terms):
        for term in terms:
            held[frozenset(key)] = held[frozenset(key)] + term.astype(FULL)

    add("pq", *(yield [send("pqx", "x")]))
    one, two, three = yield [send("pq", "q"), send("qx", "x"), send("px", "p")]
    add("p", one)
    add("q", two)
    add("x", three)
    add("", *(yield [send("p", "p"), send("q", "q"), send("x", "x")]))
    return held[frozenset()]


def gather_plane(block):
    along_x, along_q, other = yield [flip(block, "x"), flip(block, "q"), flip(block, "c")]
    corner, other_x, other_q = yield [flip(along_x, "q"), flip(along_x, "c"), flip(along_q, "c")]
    (other_corner,) = yield [flip(corner, "c")]
    return [[block, along_x, other, other_x], [along_q, corner, other_q, other_corner]]


def scatter_plane(parts):
    held = pairs_of(parts, ((), ("q",)))
    own, along_x, along_q, corner = [held[frozenset(key)] for key in ("", "x", "q", "qx")]
    (term,) = yield [flip(corner.astype(LOW), "x")]
    along_q = along_q + term.astype(FULL)
    one, two = yield [flip(along_x.astype(LOW), "x"), flip(along_q.astype(LOW), "q")]
    return own + one.astype(FULL) + two.astype(FULL)


def swap_group(blocks, axes=GROUP):
    return lax.all_to_all(blocks, axes, 0, 0, tiled=True)


def from_others(block, axis="w"):
    return [shift(block, axis, step) for step in range(1, lax.axis_size(axis))]


def put(whole, start, blocks, axis="w"):
    size, rank = lax.axis_size(axis), lax.axis_index(axis)
    for step, block in enumerate(blocks):
        index = ((rank - step) % size, start) + (0,) * (block.ndim - 1)
        whole = lax.dynamic_update_slice(whole, block[None], index)
    return whole


def rows_for(left, right, step, low, high, axis="w"):
    size, rank = lax.axis_size(axis), lax.axis_index(axis)
    rows = left.shape[1] // size
    start = ((rank - step) % size) * rows + low
    return t_product(lax.dynamic_slice_in_dim(left, start, high - low, 1), right).astype(LOW)


def to_others(terms, axis="w"):
    return [shift(term, axis, -1 - index) for index, term in enumerate(terms)]


def terms_for(left, right, low, high, axis="w"):
    steps = range(1, lax.axis_size(axis))
    return [rows_for(left, right, step, low, high, axis) for step in steps]


def added(own, received):
    total = own.astype(FULL)
    for piece in received:
        total = total + piece.astype(FULL)
    return total


def spread_kernel(places, chunk, pieces, weight_ref, gain_ref, *refs):
    gain = gain_ref[...]
    out_ref = refs[-1]
    rows = weight_ref.shape[0]
    run = chunk // pieces
    for place in range(places):
        starts = [(piece * places + place) * run for piece in range(pieces)]
        parts = [weight_ref[:, start : start + run] for start in starts]
        part = parts[0] if pieces == 1 else jnp.concatenate(parts, 1)
        out_ref[place, :rows] = (part.astype(FULL) * gain).astype(LOW)
        for ref in refs[:-1]:
            out_ref[place, rows:] = ref[...]


def spread(weight, gain, places, outer, inner, chunk, pieces=1, more=()):
    rows, _ = weight.shape
    all_rows = rows + sum(array.shape[0] for array in more)
    count = outer * inner
    if chunk % LANES or (inner > 1 and chunk != CHUNK):
        scaled = (weight.astype(FULL) * gain).astype(LOW)
        if inner > 1:
            blocks = scaled.reshape(rows, outer, inner, places, chunk).transpose(3, 0, 1, 2, 4)
            blocks = blocks.reshape(places, rows, outer, inner * chunk // CHUNK, CHUNK)
            blocks = blocks.transpose(0, 1, 3, 2, 4)
        else:
            blocks = scaled.reshape(rows, outer, places, chunk).transpose(2, 0, 1, 3)
        return blocks.reshape(places, rows, count * chunk)
    return pl.pallas_call(
        functools.partial(spread_kernel, places, chunk, pieces),
        grid=(inner, outer),
        in_specs=[
            pl.BlockSpec((rows, places * chunk), lambda i, o: (0, o * inner + i)),
            pl.BlockSpec((rows, 1), lambda i, o: (0, 0)),
        ]
        + [pl.BlockSpec(array.shape, lambda i, o: (0, 0)) for array in more],
        out_specs=pl.BlockSpec((places, all_rows, chunk), lambda i, o: (0, 0, i * outer + o)),
        out_shape=jax.ShapeDtypeStruct((places, all_rows, count * chunk), LOW),
        compiler_params=pltpu.CompilerParams(vmem_limit_bytes=VMEM_BYTES),
    )(weight, gain, *more)


def collect_kernel(places, chunk, pieces, blocks_ref, weight_ref, gain_ref, grad_ref, total_ref):
    gain = gain_ref[...]

    @pl.when((pl.program_id(0) == 0) & (pl.program_id(1) == 0))
    def _():
        total_ref[...] = jnp.zeros_like(total_ref)

    total = total_ref[...]
    run = chunk // pieces
    step = max(1, LANES // run)
    for first in range(0, places, step):
        for piece in range(pieces):
            parts = [
                blocks_ref[place, :, piece * run : (piece + 1) * run].astype(FULL)
                for place in range(first, first + step)
            ]
            part = parts[0] if step == 1 else jnp.concatenate(parts, 1)
            start = (piece * places + first) * run
            end = start + step * run
            grad_ref[:, start:end] = part * gain
            terms = part * weight_ref[:, start:end].astype(FULL)
            for lane in range(0, step * run, LANES):
                total = total + terms[:, lane : lane + LANES]
    total_ref[...] = total


def collect(blocks, weight, gain, outer, inner, chunk, pieces=1):
    places, rows, _ = blocks.shape
    columns = weight.shape[1]
    if chunk % LANES or (inner > 1 and chunk != CHUNK):
        raw = blocks.astype(FULL)
        if inner > 1:
            raw = raw.reshape(places, rows, inner * chunk // CHUNK, outer, CHUNK)
            raw = raw.transpose(0, 1, 3, 2, 4)
        raw = raw.reshape(places, rows, outer, inner, chunk).transpose(1, 2, 3, 0, 4)
        raw = raw.reshape(rows, columns)
        return raw * gain, jnp.sum(raw * weight.astype(FULL), 1)
    grad, total = pl.pallas_call(
        functools.partial(collect_kernel, places, chunk, pieces),
        grid=(inner, outer),
        in_specs=[
            pl.BlockSpec((places, rows, chunk), lambda i, o: (0, 0, i * outer + o)),
            pl.BlockSpec((rows, places * chunk), lambda i, o: (0, o * inner + i)),
            pl.BlockSpec((rows, 1), lambda i, o: (0, 0)),
        ],
        out_specs=[
            pl.BlockSpec((rows, places * chunk), lambda i, o: (0, o * inner + i)),
            pl.BlockSpec((rows, LANES), lambda i, o: (0, 0)),
        ],
        out_shape=[
            jax.ShapeDtypeStruct((rows, columns), FULL),
            jax.ShapeDtypeStruct((rows, LANES), FULL),
        ],
        compiler_params=pltpu.CompilerParams(vmem_limit_bytes=VMEM_BYTES),
    )(blocks, weight, gain)
    return grad, jnp.sum(total, 1)


def rotate(values, cosines, sines, lower):
    half_dim = HEAD_DIM // 2
    width = values.shape[-1]
    other = jnp.where(
        lower, pltpu.roll(values, width - half_dim, 1), pltpu.roll(values, half_dim, 1)
    )
    return values * cosines + other * sines


def lower_half(shape):
    return lax.broadcasted_iota(jnp.int32, shape, 1) % HEAD_DIM < HEAD_DIM // 2


def head_lanes(shape, head):
    return lax.broadcasted_iota(jnp.int32, shape, 1) // HEAD_DIM == head


def allowed_pairs(seg_col, seg_row):
    length = seg_col.shape[0]
    shape = (length, length)
    earlier = lax.broadcasted_iota(jnp.int32, shape, 1) <= lax.broadcasted_iota(jnp.int32, shape, 0)
    return earlier & (seg_row[:1, :] == seg_col[...])


def rows_at(where, index, rows):
    return pl.ds(pl.multiple_of(where[where.shape[0] - 4 + index] * rows, rows), rows)


def store_parts(where, part_ref, part_refs):
    rows = part_refs[0].shape[0]
    for index, ref in enumerate(part_refs):
        ref[...] = part_ref[rows_at(where, index, rows), :].astype(LOW)


def attend_kernel(heads, where, *refs):
    tokens_ref, weight_ref, out_weight_ref, cos_ref, sin_ref, seg_col, seg_row = refs[:7]
    scaled_ref, qkv_ref, log_ref, out_ref = refs[7:11]
    part_refs, part_ref = refs[11:15], refs[15]
    cols = heads * HEAD_DIM
    block = tokens_ref[...].astype(FULL)
    mean = jnp.mean(block * block, -1, keepdims=True)
    scaled_ref[...] = (block * lax.rsqrt(mean + EPSILON)).astype(LOW)
    mixed = product(scaled_ref[...], weight_ref[...])
    cosines, sines = cos_ref[...], sin_ref[...]
    lower = lower_half(cosines.shape)
    query = rotate(mixed[:, :cols], cosines, sines, lower).astype(LOW)
    key = rotate(mixed[:, cols : 2 * cols], cosines, sines, lower).astype(LOW)
    value = mixed[:, 2 * cols :].astype(LOW)
    qkv_ref[:, :cols] = query
    qkv_ref[:, cols : 2 * cols] = key
    qkv_ref[:, 2 * cols :] = value
    allowed = allowed_pairs(seg_col, seg_row)
    logs = jnp.zeros(query.shape, FULL)
    attended = jnp.zeros(query.shape, FULL)
    for head in range(heads):
        own = head_lanes(query.shape, head)
        scores = product_t(jnp.where(own, query, 0), key) * HEAD_DIM**-0.5
        scores = jnp.where(allowed, scores, -1e30)
        highest = jnp.max(scores, -1, keepdims=True)
        expanded = jnp.exp(scores - highest)
        denominator = jnp.sum(expanded, -1, keepdims=True)
        probs_low = (expanded / denominator).astype(LOW)
        attended = jnp.where(own, product(probs_low, value), attended)
        logs = jnp.where(own, highest + jnp.log(denominator), logs)
    log_ref[...] = logs
    out_ref[...] = attended.astype(LOW)
    part_ref[...] = product(attended.astype(LOW), out_weight_ref[...])
    store_parts(where, part_ref, part_refs)


def attend_back_kernel(heads, where, *refs):
    blocks = refs[:8]
    qkv_ref, log_ref, out_ref, weight_ref, out_weight_ref = refs[8:13]
    cos_ref, sin_ref, seg_col, seg_row = refs[13:17]
    qkv_grad_ref, part_refs, sum_ref = refs[17], refs[18:22], refs[22]
    part_ref, block_ref = refs[23:]
    rows = blocks[0].shape[0]
    for turn in range(2):

        @pl.when(pl.program_id(0) == turn)
        def _():
            for index, ref in enumerate(blocks[4 * turn : 4 * turn + 4]):
                block_ref[rows_at(where, index, rows), :] = ref[...]

    term = t_product(out_ref[...], block_ref[...])

    @pl.when(pl.program_id(0) == 0)
    def _():
        sum_ref[...] = term

    @pl.when(pl.program_id(0) > 0)
    def _():
        sum_ref[...] += term

    cols = heads * HEAD_DIM
    query = qkv_ref[:, :cols]
    key = qkv_ref[:, cols : 2 * cols]
    value = qkv_ref[:, 2 * cols :]
    grad = product_t(block_ref[...], out_weight_ref[...]).astype(LOW)
    allowed = allowed_pairs(seg_col, seg_row)
    query_grad = jnp.zeros(query.shape, FULL)
    key_grad = jnp.zeros(query.shape, FULL)
    value_grad = jnp.zeros(query.shape, FULL)
    score_scale = HEAD_DIM**-0.5
    for head in range(heads):
        own = head_lanes(query.shape, head)
        scores = product_t(jnp.where(own, query, 0), key) * score_scale
        log_total = log_ref[:, head * HEAD_DIM : head * HEAD_DIM + 1]
        probs = jnp.where(allowed, jnp.exp(jnp.where(allowed, scores - log_total, 0.0)), 0.0)
        value_grad = jnp.where(own, t_product(probs.astype(LOW), grad), value_grad)
        prob_grad = product_t(jnp.where(own, grad, 0), value)
        row_terms = jnp.sum(probs * prob_grad, -1, keepdims=True)
        score_grad = (probs * (prob_grad - row_terms)).astype(LOW)
        query_grad = jnp.where(own, product(score_grad, key), query_grad)
        key_grad = jnp.where(own, t_product(score_grad, query), key_grad)
    cosines, sines = cos_ref[...], sin_ref[...]
    lower = lower_half(cosines.shape)
    query_low = rotate(query_grad * score_scale, cosines, -sines, lower).astype(LOW)
    key_low = rotate(key_grad * score_scale, cosines, -sines, lower).astype(LOW)
    value_low = value_grad.astype(LOW)
    qkv_grad_ref[:, :cols] = query_low
    qkv_grad_ref[:, cols : 2 * cols] = key_low
    qkv_grad_ref[:, 2 * cols :] = value_low
    part = product_t(query_low, weight_ref[:, :cols])
    part = part + product_t(key_low, weight_ref[:, cols : 2 * cols])
    part = part + product_t(value_low, weight_ref[:, 2 * cols :])
    part_ref[...] = part
    store_parts(where, part_ref, part_refs)


def feed_kernel(where, *refs):
    scaled_ref, branch_ref, gate_up_ref, down_ref, hidden_ref, grad_ref = refs[:6]
    part_refs, part_ref = refs[6:10], refs[10]
    for start in range(0, down_ref.shape[0], CHUNK):
        units = slice(start, start + CHUNK)
        both = slice(2 * start, 2 * start + 2 * CHUNK)
        gate_up = product(scaled_ref[...], gate_up_ref[:, both])
        gate, upper = gate_up[:, :CHUNK], gate_up[:, CHUNK:]
        sigmoid = 1.0 / (1.0 + jnp.exp(-gate))
        silu = gate * sigmoid
        hidden_ref[:, units] = (silu * upper).astype(LOW)
        hidden_grad = product_t(branch_ref[...], down_ref[units, :])
        gate_grad = hidden_grad * upper * sigmoid * (1.0 + gate * (1.0 - sigmoid))
        grad_ref[:, 2 * start : 2 * start + CHUNK] = gate_grad.astype(LOW)
        grad_ref[:, 2 * start + CHUNK : 2 * start + 2 * CHUNK] = (hidden_grad * silu).astype(LOW)
    part_ref[...] = product_t(grad_ref[...], gate_up_ref[...])
    store_parts(where, part_ref, part_refs)


def mixed_kernel(where, hidden_ref, down_ref, *refs):
    part_refs, part_ref = refs[:4], refs[4]
    part_ref[...] = product(hidden_ref[...], down_ref[...])
    store_parts(where, part_ref, part_refs)


def on_sequences(kernel, where, operands, results, scratch, flops, exps):
    def spec(shape, rows):
        if rows > 0:
            return pl.BlockSpec((rows, *shape[1:]), lambda i, where: (where[i], 0))
        if rows < 0:
            return pl.BlockSpec((-rows, *shape[1:]), lambda i, where: (i, 0))
        return pl.BlockSpec(shape, lambda i, where: (0, 0))

    moved = sum(array.size * array.dtype.itemsize for array, _ in operands) // 16
    flops, exps = flops // 16, exps // 16
    return pl.pallas_call(
        kernel,
        grid_spec=pltpu.PrefetchScalarGridSpec(
            num_scalar_prefetch=1,
            grid=(where.shape[0] - 4,),
            in_specs=[spec(array.shape, rows) for array, rows in operands],
            out_specs=[spec(shape, rows) for (shape, _), rows in results],
            scratch_shapes=scratch,
        ),
        out_shape=[jax.ShapeDtypeStruct(shape, dtype) for (shape, dtype), _ in results],
        compiler_params=pltpu.CompilerParams(vmem_limit_bytes=VMEM_BYTES),
        cost_estimate=pl.CostEstimate(flops=flops, bytes_accessed=moved, transcendentals=exps),
    )(where, *[array for array, _ in operands])


def shards(
    tokens,
    segment_ids,
    gain_first,
    qkv_weight,
    out_weight,
    gain_second,
    gate_up_weight,
    down_weight,
    cotangent,
):
    w_size = lax.axis_size("w")
    group = 16
    p_rank, q_rank, x_rank, c_rank = (lax.axis_index(axis) for axis in GROUP)
    own_tokens = tokens[0]
    rows, width = own_tokens.shape
    length = 4 * rows
    group_rows = 4 * length
    units = down_weight.shape[0]
    own_units = w_size * units
    plane, across = 8, 2 * w_size
    plane_rows = 2 * length
    cols = width // plane
    heads = cols // HEAD_DIM

    places = [(x_rank ^ jx) * 2 + (c_rank ^ jc) for jc in range(2) for jx in range(2)]
    wheres = [(p_rank ^ jp) * 2 + (q_rank ^ jq) for jp, jq in ((0, 0), (1, 0), (0, 1), (1, 1))]
    wheres = jnp.stack(wheres + places).astype(jnp.int32)
    plane_wheres = jnp.stack([q_rank, q_rank ^ 1] + places).astype(jnp.int32)
    pieces = across if out_weight.shape[0] == HEAD_DIM else 1
    own_segments = segment_ids[0].astype(LOW).reshape(-1, cols)
    own_segments = jnp.pad(own_segments, ((0, -own_segments.shape[0] % 16), (0, 0)))
    half_dim = HEAD_DIM // 2
    freqs = jnp.exp(jnp.arange(half_dim).astype(FULL) * (-2.0 * math.log(ROPE_BASE) / HEAD_DIM))
    angles = jnp.arange(length).astype(FULL)[:, None] * freqs[None, :]
    cosines = jnp.tile(jnp.cos(angles), (1, 2 * heads))
    sines = jnp.tile(jnp.concatenate([-jnp.sin(angles), jnp.sin(angles)], 1), (1, heads))

    gain_one = gain_first.astype(FULL)[:, None]
    gain_two = gain_second.astype(FULL)[:, None]
    count = w_size - 1
    qkv_blocks = spread(qkv_weight, gain_one, plane, 3, 1, cols, pieces, [own_segments])

    tokens_all = lax.all_gather(own_tokens, PLANE, axis=0, tiled=True)
    out_received = from_others(out_weight, ACROSS) if pieces == across else []
    qkv_blocks, *out_received = together(swap_group(qkv_blocks, PLANE), *out_received)
    if pieces == across:
        out_rows = jnp.zeros((across, *out_weight.shape), LOW)
        out_rows = put(out_rows, 0, [out_weight, *out_received], ACROSS).reshape(cols, width)
    else:
        out_rows = lax.all_gather(out_weight, EVERY, axis=0, tiled=True)
        out_rows = lax.dynamic_slice_in_dim(out_rows, lax.axis_index(PLANE) * cols, cols)
    qkv_own = qkv_blocks[:, : qkv_weight.shape[0]].reshape(-1, 3 * cols)
    all_segments = qkv_blocks[::4, qkv_weight.shape[0] :].reshape(2, -1)
    all_segments = all_segments.reshape(2, -1, 3, cols)[:, :, 0].reshape(2, -1)
    all_segments = all_segments[:, :length].astype(jnp.int32)
    branch_late = after(cotangent[0], qkv_blocks)
    branch_all = lax.all_gather(branch_late, GROUP, axis=0, tiled=True)
    gate_up_late = after(gate_up_weight, qkv_blocks)
    gate_up_own = spread(gate_up_late, gain_two, group, 2, w_size, units)
    gate_up_own = swap_group(gate_up_own)
    weight_rows = group * gate_up_weight.shape[0]
    gate_up_own = gate_up_own.reshape(weight_rows, 2 * own_units)
    qkv_received = from_others(qkv_own, ACROSS)
    qkv_cols = jnp.zeros((across, *qkv_own.shape), LOW)
    qkv_cols = put(qkv_cols, 0, [qkv_own, *qkv_received], ACROSS).reshape(width, 3 * cols)
    ends = [weight_rows * i // 4 // 16 * 16 for i in range(4)] + [weight_rows]
    gate_up_parts = [gate_up_own[low:high] for low, high in zip(ends, ends[1:])]
    gate_up_cols = jnp.zeros((w_size, weight_rows, 2 * own_units), LOW)

    seg_col = all_segments.reshape(plane_rows, 1)
    seg_row = jnp.broadcast_to(all_segments[:, None], (2, 8, length)).reshape(16, length)
    down_received = from_others(after(down_weight, *qkv_received))
    scaled_ones, qkv_lows, logs, attended_heads, *out_parts = on_sequences(
        functools.partial(attend_kernel, heads),
        plane_wheres,
        [
            (tokens_all, length),
            (qkv_cols, 0),
            (out_rows, 0),
            (cosines, 0),
            (sines, 0),
            (seg_col, length),
            (seg_row, 8),
        ],
        [
            (((plane_rows, width), LOW), length),
            (((plane_rows, 3 * cols), LOW), length),
            (((plane_rows, cols), FULL), length),
            (((plane_rows, cols), LOW), length),
        ]
        + [(((2 * rows, width), LOW), -rows)] * 4,
        [pltpu.VMEM((length, width), FULL)],
        4 * length * width * 4 * cols + 8 * heads * length * length * LANES,
        2 * heads * length * length,
    )

    def norm_scale(values):
        return lax.rsqrt(jnp.mean(values * values, -1, keepdims=True) + EPSILON)

    def put_gate_up(whole, index, received):
        return put(whole, ends[index], [gate_up_parts[index], *received])

    moves = scatter_plane(out_parts)
    flips, down_received = step(moves, next(moves), down_received)
    out_sum, received = step(moves, flips, from_others(after(gate_up_parts[0], *down_received)))
    gate_up_cols = put_gate_up(gate_up_cols, 0, received)
    inputs = own_tokens.astype(FULL)
    residual = inputs + out_sum
    inverse_two = norm_scale(residual)
    scaled_two = residual * inverse_two
    scaled_twos = lax.all_gather(scaled_two.astype(LOW), GROUP, axis=0, tiled=True)
    for index in range(1, 4):
        received = from_others(after(gate_up_parts[index], *received))
        gate_up_cols = put_gate_up(gate_up_cols, index, received)
    gate_up_cols = gate_up_cols.reshape(width, 2 * own_units)
    down_rows = jnp.zeros((w_size, units, width), LOW)
    down_rows = put(down_rows, 0, [down_weight, *down_received]).reshape(own_units, width)

    hiddens, gate_up_grads, *two_parts = on_sequences(
        feed_kernel,
        wheres,
        [(scaled_twos, length), (branch_all, length), (gate_up_cols, 0), (down_rows, 0)],
        [
            (((group_rows, own_units), LOW), length),
            (((group_rows, 2 * own_units), LOW), length),
        ]
        + [(((4 * rows, width), LOW), -rows)] * 4,
        [pltpu.VMEM((length, width), FULL)],
        40 * length * width * own_units,
        4 * length * own_units,
    )

    def gate_up_terms(left, index):
        return terms_for(left, gate_up_grads, ends[index], ends[index + 1])

    def halves(terms):
        return [[term[: units // 2] for term in terms], [term[units // 2 :] for term in terms]]

    moves = scatter_steps(two_parts)
    down_terms = halves(terms_for(hiddens, branch_all, 0, units))
    flips, down_first = step(moves, next(moves), to_others(down_terms[0]))
    late_scaled = after(scaled_twos, *down_terms[0])
    all_terms = [gate_up_terms(late_scaled, index) for index in range(2)]
    flips, down_second = step(moves, flips, to_others(down_terms[1]))
    weighted_two, received = step(moves, flips, to_others(all_terms[0]))
    gate_up_received = [received]
    upstream = cotangent[0].astype(FULL)
    residual_grad = upstream + inverse_two * (
        weighted_two - scaled_two * jnp.mean(weighted_two * scaled_two, -1, keepdims=True)
    )
    attn_grad_low = residual_grad.astype(LOW)
    late_scaled = after(scaled_twos, attn_grad_low)
    all_terms += [gate_up_terms(late_scaled, index) for index in range(2, 4)]
    moves = gather_plane(attn_grad_low)
    for index in range(1, 3):
        flips, beside = step(
            moves,
            flips if index > 1 else next(moves),
            [*to_others(all_terms[index]), *all_terms[3]],
        )
        gate_up_received.append(beside[:count])
        all_terms[3] = beside[count:]
    gate_up_received.append(to_others(all_terms[3]))
    grad_blocks, _ = step(moves, flips)
    qkv_grads, *one_parts, out_sum = on_sequences(
        functools.partial(attend_back_kernel, heads),
        plane_wheres,
        [(block, 0) for blocks in grad_blocks for block in blocks]
        + [(qkv_lows, length), (logs, length), (attended_heads, length)]
        + [(array, 0) for array in (qkv_cols, out_rows, cosines, sines)]
        + [(seg_col, length), (seg_row, 8)],
        [(((plane_rows, 3 * cols), LOW), length)]
        + [(((2 * rows, width), LOW), -rows)] * 4
        + [(((cols, width), FULL), 0)],
        [pltpu.VMEM((length, width), FULL), pltpu.VMEM((length, width), LOW)],
        4 * length * width * 5 * cols + 20 * heads * length * length * LANES,
        2 * heads * length * length,
    )
    late_scaled, late_hiddens, late_ones = after((scaled_twos, hiddens, scaled_ones), qkv_grads)
    qkv_terms = terms_for(late_ones, qkv_grads, 0, width // across, ACROSS)
    gate_up_own = rows_for(late_scaled, gate_up_grads, 0, 0, weight_rows)
    moves = scatter_plane(one_parts)
    rank = lax.axis_index(ACROSS)
    out_part = out_sum.reshape(across, cols // across, width)
    out_part, *out_terms = [
        lax.dynamic_index_in_dim(out_part, (rank - step) % across, 0, keepdims=False)
        for step in range(across)
    ]
    flips, beside = step(moves, next(moves), [*gate_up_received[3], *qkv_terms, gate_up_own])
    gate_up_received[3] = beside[:count]
    qkv_terms, gate_up_own = beside[count:-1], beside[-1]
    weighted_one, qkv_received = step(moves, flips, to_others(qkv_terms, ACROSS))
    gate_up_received = [jnp.concatenate(parts, 0) for parts in zip(*gate_up_received)]
    gate_up_mine = added(gate_up_own, gate_up_received)
    mixed_parts = on_sequences(
        mixed_kernel,
        wheres,
        [(late_hiddens, length), (down_rows, 0)],
        [(((4 * rows, width), LOW), -rows)] * 4,
        [pltpu.VMEM((length, width), FULL)],
        8 * length * width * own_units,
        0,
    )
    mixed_moves = scatter_steps(mixed_parts)
    qkv_own = rows_for(late_ones, qkv_grads, 0, 0, width // across, ACROSS)
    down_own = rows_for(late_hiddens, branch_all, 0, 0, units)
    mixed_flips, _ = step(mixed_moves, next(mixed_moves))
    mixed_flips, _ = step(mixed_moves, mixed_flips)
    mixed_sum, _ = step(mixed_moves, mixed_flips)
    mixed = (residual + mixed_sum).astype(LOW)
    qkv_mine = added(qkv_own, qkv_received)
    down_grad = added(
        down_own, [jnp.concatenate(parts, 0) for parts in zip(down_first, down_second)]
    )
    out_terms = after([term.astype(LOW) for term in out_terms], *qkv_received)
    out_grad = added(out_part, to_others(out_terms, ACROSS))
    if pieces != across:
        owners = [(z * plane + t, t * across + z) for z in range(across) for t in range(plane)]
        out_grad = lax.ppermute(out_grad.astype(LOW), EVERY, owners).astype(FULL)

    def to_owners(mine, places, axes):
        return swap_group(mine.astype(LOW).reshape(places, -1, mine.shape[-1]), axes)

    gate_up_blocks = to_owners(gate_up_mine, group, GROUP)
    qkv_blocks = to_owners(after(qkv_mine, gate_up_blocks), plane, PLANE)

    inverse_one = norm_scale(inputs)
    scaled_one = inputs * inverse_one
    input_grad = residual_grad + inverse_one * (
        weighted_one - scaled_one * jnp.mean(weighted_one * scaled_one, -1, keepdims=True)
    )
    gate_up_grad, gain_two_grad = collect(
        gate_up_blocks, gate_up_weight, gain_two, 2, w_size, units
    )
    qkv_grad, gain_one_grad = collect(qkv_blocks, qkv_weight, gain_one, 3, 1, cols, pieces)
    return (
        mixed[None],
        input_grad[None],
        gain_one_grad,
        qkv_grad,
        out_grad,
        gain_two_grad,
        gate_up_grad,
        down_grad,
    )


def solution(mesh):
    dp_size, _ = mesh.devices.shape
    fine = Mesh(mesh.devices.reshape(dp_size // 4, 2, 2, 2, 2), EVERY)
    token_spec = P(("w", "p", "q"), ("x", "c"), None)
    matrix, vector = P(EVERY, None), P(EVERY)
    return jax.shard_map(
        shards,
        mesh=fine,
        in_specs=(
            token_spec,
            P(("w", "p", "q"), None),
            vector,
            matrix,
            matrix,
            vector,
            matrix,
            matrix,
            token_spec,
        ),
        out_specs=(token_spec, token_spec, vector, matrix, matrix, vector, matrix, matrix),
        check_vma=False,
    )
```

```python
import functools
import math

import jax
import jax.numpy as jnp
from jax import lax
from jax.experimental import pallas as pl
from jax.experimental.pallas import tpu as pltpu
from jax.sharding import Mesh, PartitionSpec as P

HEAD_DIM = 64
EPSILON = 1e-05
ROPE_BASE = 130000.0
LANES = 128
LOW = jnp.bfloat16
FULL = jnp.float32
VMEM_BYTES = 50 * 1024 * 1024

CHUNK = 256

CUBE = ("p", "q", "x")
GROUP = ("p", "q", "x", "c")
PLANE = ("q", "x", "c")
ACROSS = ("w", "p")
EVERY = ("w", "p", "q", "x", "c")


def shift(value, axis, step):
    size = lax.axis_size(axis)
    if step % size == 0:
        return value
    return lax.ppermute(value, axis, [(i, (i + step) % size) for i in range(size)])


def flip(value, axis):
    return shift(value, axis, 1)


def together(*values):
    return lax.optimization_barrier(values)


def after(value, *earlier):
    return lax.optimization_barrier((value,) + earlier)[0]


def product(left, right):
    return jnp.dot(left, right, preferred_element_type=FULL)


def product_t(left, right):
    return lax.dot_general(left, right, (((1,), (1,)), ((), ())), preferred_element_type=FULL)


def t_product(left, right):
    return lax.dot_general(left, right, (((0,), (0,)), ((), ())), preferred_element_type=FULL)


SEQUENCES = ((), ("p",), ("q",), ("p", "q"))


def step(moves, flips, beside=()):
    values = together(*flips, *beside)
    try:
        later = moves.send(values[: len(flips)])
    except StopIteration as end:
        later = end.value
    return later, values[len(flips) :]


def pairs_of(parts, sequences):
    rows = parts[0].shape[0] // len(sequences)
    held = {}
    for index, along_x in enumerate(((), ("x",))):
        other = flip(parts[2 + index], "c")
        for row, place in enumerate(sequences):
            own = slice(row * rows, (row + 1) * rows)
            held[frozenset(place + along_x)] = parts[index][own].astype(FULL) + other[own].astype(
                FULL
            )
    return held


def scatter_steps(parts):
    held = pairs_of(parts, SEQUENCES)

    def send(key, axis):
        return flip(held[frozenset(key)].astype(LOW), axis)

    def add(key, *terms):
        for term in terms:
            held[frozenset(key)] = held[frozenset(key)] + term.astype(FULL)

    add("pq", *(yield [send("pqx", "x")]))
    one, two, three = yield [send("pq", "q"), send("qx", "x"), send("px", "p")]
    add("p", one)
    add("q", two)
    add("x", three)
    add("", *(yield [send("p", "p"), send("q", "q"), send("x", "x")]))
    return held[frozenset()]


def gather_plane(block):
    along_x, along_q, other = yield [flip(block, "x"), flip(block, "q"), flip(block, "c")]
    corner, other_x, other_q = yield [flip(along_x, "q"), flip(along_x, "c"), flip(along_q, "c")]
    (other_corner,) = yield [flip(corner, "c")]
    return [[block, along_x, other, other_x], [along_q, corner, other_q, other_corner]]


def scatter_plane(parts):
    held = pairs_of(parts, ((), ("q",)))
    own, along_x, along_q, corner = [held[frozenset(key)] for key in ("", "x", "q", "qx")]
    (term,) = yield [flip(corner.astype(LOW), "x")]
    along_q = along_q + term.astype(FULL)
    one, two = yield [flip(along_x.astype(LOW), "x"), flip(along_q.astype(LOW), "q")]
    return own + one.astype(FULL) + two.astype(FULL)


def swap_group(blocks, axes=GROUP):
    return lax.all_to_all(blocks, axes, 0, 0, tiled=True)


def from_others(block, axis="w"):
    return [shift(block, axis, step) for step in range(1, lax.axis_size(axis))]


def put(whole, start, blocks, axis="w"):
    size, rank = lax.axis_size(axis), lax.axis_index(axis)
    for step, block in enumerate(blocks):
        index = ((rank - step) % size, start) + (0,) * (block.ndim - 1)
        whole = lax.dynamic_update_slice(whole, block[None], index)
    return whole


def rows_for(left, right, step, low, high, axis="w"):
    size, rank = lax.axis_size(axis), lax.axis_index(axis)
    rows = left.shape[1] // size
    start = ((rank - step) % size) * rows + low
    return t_product(lax.dynamic_slice_in_dim(left, start, high - low, 1), right).astype(LOW)


def to_others(terms, axis="w"):
    return [shift(term, axis, -1 - index) for index, term in enumerate(terms)]


def terms_for(left, right, low, high, axis="w"):
    steps = range(1, lax.axis_size(axis))
    return [rows_for(left, right, step, low, high, axis) for step in steps]


def added(own, received):
    total = own.astype(FULL)
    for piece in received:
        total = total + piece.astype(FULL)
    return total


def spread_kernel(places, chunk, pieces, weight_ref, gain_ref, *refs):
    gain = gain_ref[...]
    out_ref = refs[-1]
    rows = weight_ref.shape[0]
    run = chunk // pieces
    for place in range(places):
        starts = [(piece * places + place) * run for piece in range(pieces)]
        parts = [weight_ref[:, start : start + run] for start in starts]
        part = parts[0] if pieces == 1 else jnp.concatenate(parts, 1)
        out_ref[place, :rows] = (part.astype(FULL) * gain).astype(LOW)
        for ref in refs[:-1]:
            out_ref[place, rows:] = ref[...]


def spread(weight, gain, places, outer, inner, chunk, pieces=1, more=()):
    rows, _ = weight.shape
    all_rows = rows + sum(array.shape[0] for array in more)
    count = outer * inner
    if chunk % LANES or (inner > 1 and chunk != CHUNK):
        scaled = (weight.astype(FULL) * gain).astype(LOW)
        if inner > 1:
            blocks = scaled.reshape(rows, outer, inner, places, chunk).transpose(3, 0, 1, 2, 4)
            blocks = blocks.reshape(places, rows, outer, inner * chunk // CHUNK, CHUNK)
            blocks = blocks.transpose(0, 1, 3, 2, 4)
        else:
            blocks = scaled.reshape(rows, outer, places, chunk).transpose(2, 0, 1, 3)
        return blocks.reshape(places, rows, count * chunk)
    return pl.pallas_call(
        functools.partial(spread_kernel, places, chunk, pieces),
        grid=(inner, outer),
        in_specs=[
            pl.BlockSpec((rows, places * chunk), lambda i, o: (0, o * inner + i)),
            pl.BlockSpec((rows, 1), lambda i, o: (0, 0)),
        ]
        + [pl.BlockSpec(array.shape, lambda i, o: (0, 0)) for array in more],
        out_specs=pl.BlockSpec((places, all_rows, chunk), lambda i, o: (0, 0, i * outer + o)),
        out_shape=jax.ShapeDtypeStruct((places, all_rows, count * chunk), LOW),
        compiler_params=pltpu.CompilerParams(vmem_limit_bytes=VMEM_BYTES),
    )(weight, gain, *more)


def collect_kernel(places, chunk, pieces, blocks_ref, weight_ref, gain_ref, grad_ref, total_ref):
    gain = gain_ref[...]

    @pl.when((pl.program_id(0) == 0) & (pl.program_id(1) == 0))
    def _():
        total_ref[...] = jnp.zeros_like(total_ref)

    total = total_ref[...]
    run = chunk // pieces
    step = max(1, LANES // run)
    for first in range(0, places, step):
        for piece in range(pieces):
            parts = [
                blocks_ref[place, :, piece * run : (piece + 1) * run].astype(FULL)
                for place in range(first, first + step)
            ]
            part = parts[0] if step == 1 else jnp.concatenate(parts, 1)
            start = (piece * places + first) * run
            end = start + step * run
            grad_ref[:, start:end] = part * gain
            terms = part * weight_ref[:, start:end].astype(FULL)
            for lane in range(0, step * run, LANES):
                total = total + terms[:, lane : lane + LANES]
    total_ref[...] = total


def collect(blocks, weight, gain, outer, inner, chunk, pieces=1):
    places, rows, _ = blocks.shape
    columns = weight.shape[1]
    if chunk % LANES or (inner > 1 and chunk != CHUNK):
        raw = blocks.astype(FULL)
        if inner > 1:
            raw = raw.reshape(places, rows, inner * chunk // CHUNK, outer, CHUNK)
            raw = raw.transpose(0, 1, 3, 2, 4)
        raw = raw.reshape(places, rows, outer, inner, chunk).transpose(1, 2, 3, 0, 4)
        raw = raw.reshape(rows, columns)
        return raw * gain, jnp.sum(raw * weight.astype(FULL), 1)
    grad, total = pl.pallas_call(
        functools.partial(collect_kernel, places, chunk, pieces),
        grid=(inner, outer),
        in_specs=[
            pl.BlockSpec((places, rows, chunk), lambda i, o: (0, 0, i * outer + o)),
            pl.BlockSpec((rows, places * chunk), lambda i, o: (0, o * inner + i)),
            pl.BlockSpec((rows, 1), lambda i, o: (0, 0)),
        ],
        out_specs=[
            pl.BlockSpec((rows, places * chunk), lambda i, o: (0, o * inner + i)),
            pl.BlockSpec((rows, LANES), lambda i, o: (0, 0)),
        ],
        out_shape=[
            jax.ShapeDtypeStruct((rows, columns), FULL),
            jax.ShapeDtypeStruct((rows, LANES), FULL),
        ],
        compiler_params=pltpu.CompilerParams(vmem_limit_bytes=VMEM_BYTES),
    )(blocks, weight, gain)
    return grad, jnp.sum(total, 1)


def rotate(values, cosines, sines, lower):
    half_dim = HEAD_DIM // 2
    width = values.shape[-1]
    other = jnp.where(
        lower, pltpu.roll(values, width - half_dim, 1), pltpu.roll(values, half_dim, 1)
    )
    return values * cosines + other * sines


def lower_half(shape):
    return lax.broadcasted_iota(jnp.int32, shape, 1) % HEAD_DIM < HEAD_DIM // 2


def head_lanes(shape, head):
    return lax.broadcasted_iota(jnp.int32, shape, 1) // HEAD_DIM == head


def allowed_pairs(seg_col, seg_row):
    length = seg_col.shape[0]
    shape = (length, length)
    earlier = lax.broadcasted_iota(jnp.int32, shape, 1) <= lax.broadcasted_iota(jnp.int32, shape, 0)
    return earlier & (seg_row[:1, :] == seg_col[...])


def rows_at(where, index, rows):
    return pl.ds(pl.multiple_of(where[where.shape[0] - 4 + index] * rows, rows), rows)


def store_parts(where, part_ref, part_refs):
    rows = part_refs[0].shape[0]
    for index, ref in enumerate(part_refs):
        ref[...] = part_ref[rows_at(where, index, rows), :].astype(LOW)


def attend_kernel(heads, where, *refs):
    tokens_ref, weight_ref, out_weight_ref, cos_ref, sin_ref, seg_col, seg_row = refs[:7]
    scaled_ref, qkv_ref, log_ref, out_ref = refs[7:11]
    part_refs, part_ref = refs[11:15], refs[15]
    cols = heads * HEAD_DIM
    block = tokens_ref[...].astype(FULL)
    mean = jnp.mean(block * block, -1, keepdims=True)
    scaled_ref[...] = (block * lax.rsqrt(mean + EPSILON)).astype(LOW)
    mixed = product(scaled_ref[...], weight_ref[...])
    cosines, sines = cos_ref[...], sin_ref[...]
    lower = lower_half(cosines.shape)
    query = rotate(mixed[:, :cols], cosines, sines, lower).astype(LOW)
    key = rotate(mixed[:, cols : 2 * cols], cosines, sines, lower).astype(LOW)
    value = mixed[:, 2 * cols :].astype(LOW)
    qkv_ref[:, :cols] = query
    qkv_ref[:, cols : 2 * cols] = key
    qkv_ref[:, 2 * cols :] = value
    allowed = allowed_pairs(seg_col, seg_row)
    logs = jnp.zeros(query.shape, FULL)
    attended = jnp.zeros(query.shape, FULL)
    for head in range(heads):
        own = head_lanes(query.shape, head)
        scores = product_t(jnp.where(own, query, 0), key) * HEAD_DIM**-0.5
        scores = jnp.where(allowed, scores, -1e30)
        highest = jnp.max(scores, -1, keepdims=True)
        expanded = jnp.exp(scores - highest)
        denominator = jnp.sum(expanded, -1, keepdims=True)
        probs_low = (expanded / denominator).astype(LOW)
        attended = jnp.where(own, product(probs_low, value), attended)
        logs = jnp.where(own, highest + jnp.log(denominator), logs)
    log_ref[...] = logs
    out_ref[...] = attended.astype(LOW)
    part_ref[...] = product(attended.astype(LOW), out_weight_ref[...])
    store_parts(where, part_ref, part_refs)


def attend_back_kernel(heads, where, *refs):
    blocks = refs[:8]
    qkv_ref, log_ref, out_ref, weight_ref, out_weight_ref = refs[8:13]
    cos_ref, sin_ref, seg_col, seg_row = refs[13:17]
    qkv_grad_ref, part_ref, sum_ref, block_ref = refs[17:]
    rows = blocks[0].shape[0]
    for turn in range(2):

        @pl.when(pl.program_id(0) == turn)
        def _():
            for index, ref in enumerate(blocks[4 * turn : 4 * turn + 4]):
                block_ref[rows_at(where, index, rows), :] = ref[...]

    term = t_product(out_ref[...], block_ref[...])

    @pl.when(pl.program_id(0) == 0)
    def _():
        sum_ref[...] = term

    @pl.when(pl.program_id(0) > 0)
    def _():
        sum_ref[...] += term

    cols = heads * HEAD_DIM
    query = qkv_ref[:, :cols]
    key = qkv_ref[:, cols : 2 * cols]
    value = qkv_ref[:, 2 * cols :]
    grad = product_t(block_ref[...], out_weight_ref[...]).astype(LOW)
    allowed = allowed_pairs(seg_col, seg_row)
    query_grad = jnp.zeros(query.shape, FULL)
    key_grad = jnp.zeros(query.shape, FULL)
    value_grad = jnp.zeros(query.shape, FULL)
    score_scale = HEAD_DIM**-0.5
    for head in range(heads):
        own = head_lanes(query.shape, head)
        scores = product_t(jnp.where(own, query, 0), key) * score_scale
        log_total = log_ref[:, head * HEAD_DIM : head * HEAD_DIM + 1]
        probs = jnp.where(allowed, jnp.exp(jnp.where(allowed, scores - log_total, 0.0)), 0.0)
        value_grad = jnp.where(own, t_product(probs.astype(LOW), grad), value_grad)
        prob_grad = product_t(jnp.where(own, grad, 0), value)
        row_terms = jnp.sum(probs * prob_grad, -1, keepdims=True)
        score_grad = (probs * (prob_grad - row_terms)).astype(LOW)
        query_grad = jnp.where(own, product(score_grad, key), query_grad)
        key_grad = jnp.where(own, t_product(score_grad, query), key_grad)
    cosines, sines = cos_ref[...], sin_ref[...]
    lower = lower_half(cosines.shape)
    query_low = rotate(query_grad * score_scale, cosines, -sines, lower).astype(LOW)
    key_low = rotate(key_grad * score_scale, cosines, -sines, lower).astype(LOW)
    value_low = value_grad.astype(LOW)
    qkv_grad_ref[:, :cols] = query_low
    qkv_grad_ref[:, cols : 2 * cols] = key_low
    qkv_grad_ref[:, 2 * cols :] = value_low
    part = product_t(query_low, weight_ref[:, :cols])
    part = part + product_t(key_low, weight_ref[:, cols : 2 * cols])
    part = part + product_t(value_low, weight_ref[:, 2 * cols :])
    part_ref[...] = part.astype(LOW)


def feed_kernel(where, *refs):
    scaled_ref, branch_ref, gate_up_ref, down_ref, hidden_ref, grad_ref = refs[:6]
    part_refs, part_ref = refs[6:10], refs[10]
    branch = branch_ref[...].reshape(scaled_ref.shape)
    for start in range(0, down_ref.shape[0], CHUNK):
        units = slice(start, start + CHUNK)
        both = slice(2 * start, 2 * start + 2 * CHUNK)
        gate_up = product(scaled_ref[...], gate_up_ref[:, both])
        gate, upper = gate_up[:, :CHUNK], gate_up[:, CHUNK:]
        sigmoid = 1.0 / (1.0 + jnp.exp(-gate))
        silu = gate * sigmoid
        hidden = (silu * upper).astype(LOW)
        hidden_ref[:, :, :, units] = hidden.reshape(*hidden_ref.shape[:3], CHUNK)
        hidden_grad = product_t(branch, down_ref[units, :])
        gate_grad = hidden_grad * upper * sigmoid * (1.0 + gate * (1.0 - sigmoid))
        grad_ref[:, 2 * start : 2 * start + CHUNK] = gate_grad.astype(LOW)
        grad_ref[:, 2 * start + CHUNK : 2 * start + 2 * CHUNK] = (hidden_grad * silu).astype(LOW)
    part_ref[...] = product_t(grad_ref[...], gate_up_ref[...])
    store_parts(where, part_ref, part_refs)


def on_sequences(kernel, where, operands, results, scratch, flops, exps):
    def spec(shape, rows):
        if isinstance(rows, tuple):
            return pl.BlockSpec(*rows)
        if rows > 0:
            return pl.BlockSpec((rows, *shape[1:]), lambda i, where: (where[i], 0))
        if rows < 0:
            return pl.BlockSpec((-rows, *shape[1:]), lambda i, where: (i, 0))
        return pl.BlockSpec(shape, lambda i, where: (0, 0))

    moved = sum(array.size * array.dtype.itemsize for array, _ in operands) // 16
    flops, exps = flops // 16, exps // 16
    return pl.pallas_call(
        kernel,
        grid_spec=pltpu.PrefetchScalarGridSpec(
            num_scalar_prefetch=1,
            grid=(where.shape[0] - 4,),
            in_specs=[spec(array.shape, rows) for array, rows in operands],
            out_specs=[spec(shape, rows) for (shape, _), rows in results],
            scratch_shapes=scratch,
        ),
        out_shape=[jax.ShapeDtypeStruct(shape, dtype) for (shape, dtype), _ in results],
        compiler_params=pltpu.CompilerParams(vmem_limit_bytes=VMEM_BYTES),
        cost_estimate=pl.CostEstimate(flops=flops, bytes_accessed=moved, transcendentals=exps),
    )(where, *[array for array, _ in operands])


def shards(
    tokens,
    segment_ids,
    gain_first,
    qkv_weight,
    out_weight,
    gain_second,
    gate_up_weight,
    down_weight,
    cotangent,
):
    w_size = lax.axis_size("w")
    group = 16
    p_rank, q_rank, x_rank, c_rank = (lax.axis_index(axis) for axis in GROUP)
    own_tokens = tokens[0]
    rows, width = own_tokens.shape
    length = 4 * rows
    group_rows = 4 * length
    units = down_weight.shape[0]
    own_units = w_size * units
    plane, across = 8, 2 * w_size
    plane_rows = 2 * length
    cols = width // plane
    heads = cols // HEAD_DIM

    places = [(x_rank ^ jx) * 2 + (c_rank ^ jc) for jc in range(2) for jx in range(2)]
    wheres = [(p_rank ^ jp) * 2 + (q_rank ^ jq) for jp, jq in ((0, 0), (1, 0), (0, 1), (1, 1))]
    wheres = jnp.stack(wheres + places).astype(jnp.int32)
    cube_spec = ((4, 1, rows, width), lambda i, where: (where[i] % 2, i % 2, 0, 0))
    unit_spec = ((4, 1, rows, own_units), cube_spec[1])
    plane_wheres = jnp.stack([q_rank, q_rank ^ 1] + places).astype(jnp.int32)
    pieces = across if out_weight.shape[0] == HEAD_DIM else 1
    own_segments = segment_ids[0].astype(LOW).reshape(-1, cols)
    own_segments = jnp.pad(own_segments, ((0, -own_segments.shape[0] % 16), (0, 0)))
    half_dim = HEAD_DIM // 2
    freqs = jnp.exp(jnp.arange(half_dim).astype(FULL) * (-2.0 * math.log(ROPE_BASE) / HEAD_DIM))
    angles = jnp.arange(length).astype(FULL)[:, None] * freqs[None, :]
    cosines = jnp.tile(jnp.cos(angles), (1, 2 * heads))
    sines = jnp.tile(jnp.concatenate([-jnp.sin(angles), jnp.sin(angles)], 1), (1, heads))

    gain_one = gain_first.astype(FULL)[:, None]
    gain_two = gain_second.astype(FULL)[:, None]
    count = w_size - 1
    qkv_blocks = spread(qkv_weight, gain_one, plane, 3, 1, cols, pieces, [own_segments])

    tokens_all = lax.all_gather(own_tokens, PLANE, axis=0, tiled=True)
    out_received = from_others(out_weight, ACROSS) if pieces == across else []
    qkv_blocks, branch_pair, *out_received = together(
        swap_group(qkv_blocks, PLANE), flip(cotangent[0], "p"), *out_received
    )
    if pieces == across:
        out_rows = jnp.zeros((across, *out_weight.shape), LOW)
        out_rows = put(out_rows, 0, [out_weight, *out_received], ACROSS).reshape(cols, width)
    else:
        out_rows = lax.all_gather(out_weight, EVERY, axis=0, tiled=True)
        out_rows = lax.dynamic_slice_in_dim(out_rows, lax.axis_index(PLANE) * cols, cols)
    qkv_own = qkv_blocks[:, : qkv_weight.shape[0]].reshape(-1, 3 * cols)
    all_segments = qkv_blocks[::4, qkv_weight.shape[0] :].reshape(2, -1)
    all_segments = all_segments.reshape(2, -1, 3, cols)[:, :, 0].reshape(2, -1)
    all_segments = all_segments[:, :length].astype(jnp.int32)
    branch_all = lax.all_gather(jnp.stack([cotangent[0], branch_pair]), PLANE)
    gate_up_late = after(gate_up_weight, qkv_blocks)
    gate_up_own = spread(gate_up_late, gain_two, group, 2, w_size, units)
    gate_up_own = swap_group(gate_up_own)
    weight_rows = group * gate_up_weight.shape[0]
    gate_up_own = gate_up_own.reshape(weight_rows, 2 * own_units)
    qkv_received = from_others(qkv_own, ACROSS)
    qkv_cols = jnp.zeros((across, *qkv_own.shape), LOW)
    qkv_cols = put(qkv_cols, 0, [qkv_own, *qkv_received], ACROSS).reshape(width, 3 * cols)
    ends = [weight_rows * i // 4 // 16 * 16 for i in range(4)] + [weight_rows]
    gate_up_parts = [gate_up_own[low:high] for low, high in zip(ends, ends[1:])]
    gate_up_cols = jnp.zeros((w_size, weight_rows, 2 * own_units), LOW)

    seg_col = all_segments.reshape(plane_rows, 1)
    seg_row = jnp.broadcast_to(all_segments[:, None], (2, 8, length)).reshape(16, length)
    scaled_ones, qkv_lows, logs, attended_heads, *out_parts = on_sequences(
        functools.partial(attend_kernel, heads),
        plane_wheres,
        [
            (tokens_all, length),
            (qkv_cols, 0),
            (out_rows, 0),
            (cosines, 0),
            (sines, 0),
            (seg_col, length),
            (seg_row, 8),
        ],
        [
            (((plane_rows, width), LOW), length),
            (((plane_rows, 3 * cols), LOW), length),
            (((plane_rows, cols), FULL), length),
            (((plane_rows, cols), LOW), length),
        ]
        + [(((2 * rows, width), LOW), -rows)] * 4,
        [pltpu.VMEM((length, width), FULL)],
        4 * length * width * 4 * cols + 8 * heads * length * length * LANES,
        2 * heads * length * length,
    )

    def norm_scale(values):
        return lax.rsqrt(jnp.mean(values * values, -1, keepdims=True) + EPSILON)

    def put_gate_up(whole, index, received):
        return put(whole, ends[index], [gate_up_parts[index], *received])

    moves = scatter_plane(out_parts)
    half = units // 2
    down_late = after(down_weight, *qkv_received)
    flips, down_first = step(moves, next(moves), from_others(down_late[:half]))
    out_sum, beside = step(
        moves, flips, [*from_others(after(down_late[half:], *down_first)), *gate_up_parts]
    )
    received, gate_up_parts = beside[:count], beside[count:]
    down_others = [jnp.concatenate(parts, 0) for parts in zip(down_first, received)]
    inputs = own_tokens.astype(FULL)
    residual = inputs + out_sum
    inverse_two = norm_scale(residual)
    scaled_two = residual * inverse_two
    scaled_twos = lax.all_gather(scaled_two.astype(LOW), GROUP, axis=0, tiled=True)
    for index in range(4):
        received = from_others(after(gate_up_parts[index], *received))
        gate_up_cols = put_gate_up(gate_up_cols, index, received)
    gate_up_cols = gate_up_cols.reshape(width, 2 * own_units)
    down_rows = jnp.zeros((w_size, units, width), LOW)
    down_rows = put(down_rows, 0, [down_weight, *down_others]).reshape(own_units, width)

    unit_rows, gate_up_grads, *two_parts = on_sequences(
        feed_kernel,
        wheres,
        [(scaled_twos, length), (branch_all, cube_spec), (gate_up_cols, 0), (down_rows, 0)],
        [
            (((plane, 2, rows, own_units), LOW), unit_spec),
            (((group_rows, 2 * own_units), LOW), length),
        ]
        + [(((4 * rows, width), LOW), -rows)] * 4,
        [pltpu.VMEM((length, width), FULL)],
        40 * length * width * own_units,
        4 * length * own_units,
    )

    hiddens = unit_rows.reshape(group_rows, own_units)
    branch_rows = branch_all.reshape(group_rows, width)

    def gate_up_terms(left, index):
        return terms_for(left, gate_up_grads, ends[index], ends[index + 1])

    def halves(terms):
        return [[term[: units // 2] for term in terms], [term[units // 2 :] for term in terms]]

    moves = scatter_steps(two_parts)
    down_terms = halves(terms_for(hiddens, branch_rows, 0, units))
    late_scaled = after(scaled_twos, *down_terms[0])
    all_terms = [gate_up_terms(late_scaled, index) for index in range(4)]
    flips, beside = step(
        moves,
        next(moves),
        [*to_others(down_terms[0]), *[term for terms in all_terms for term in terms]],
    )
    down_first = beside[:count]
    all_terms = [beside[i * count : i * count + count] for i in range(1, 5)]
    mixed_term = product(after(hiddens, flips), down_rows).astype(LOW)
    flips, beside = step(moves, flips, [*to_others(down_terms[1]), mixed_term])
    down_second = beside[:count]
    mixed_sum = lax.psum_scatter(beside[count], PLANE, scatter_dimension=0, tiled=True)
    gate_up_own = rows_for(after(scaled_twos, flips), gate_up_grads, 0, 0, weight_rows)
    weighted_two, beside = step(moves, flips, [*to_others(all_terms[0]), gate_up_own])
    gate_up_received, gate_up_own = [beside[:count]], beside[count]
    upstream = cotangent[0].astype(FULL)
    residual_grad = upstream + inverse_two * (
        weighted_two - scaled_two * jnp.mean(weighted_two * scaled_two, -1, keepdims=True)
    )
    attn_grad_low = residual_grad.astype(LOW)
    moves = gather_plane(attn_grad_low)
    flips, received = step(moves, next(moves), to_others(all_terms[1]))
    gate_up_received.append(received)
    flips, received = step(moves, flips, to_others(all_terms[2]))
    gate_up_received += [received, to_others(all_terms[3])]
    grad_blocks, _ = step(moves, flips)
    qkv_grads, one_term, out_sum = on_sequences(
        functools.partial(attend_back_kernel, heads),
        plane_wheres,
        [(block, 0) for blocks in grad_blocks for block in blocks]
        + [(qkv_lows, length), (logs, length), (attended_heads, length)]
        + [(array, 0) for array in (qkv_cols, out_rows, cosines, sines)]
        + [(seg_col, length), (seg_row, 8)],
        [
            (((plane_rows, 3 * cols), LOW), length),
            (((plane_rows, width), LOW), length),
            (((cols, width), FULL), 0),
        ],
        [pltpu.VMEM((length, width), LOW)],
        4 * length * width * 5 * cols + 20 * heads * length * length * LANES,
        2 * heads * length * length,
    )
    qkv_grads, one_term, out_sum, *received = together(
        qkv_grads, one_term, out_sum, *gate_up_received[3]
    )
    gate_up_received[3] = received
    mixed_rows = after(mixed_sum, qkv_grads)
    mixed_sum = added(mixed_rows[:rows], [flip(mixed_rows[rows:], "p")])
    mixed = (residual + mixed_sum).astype(LOW)
    late_ones = after(scaled_ones, qkv_grads)
    qkv_terms = terms_for(late_ones, qkv_grads, 0, width // across, ACROSS)
    late_hiddens = after(hiddens, *qkv_terms)
    one_term = after(one_term, mixed_rows)
    weighted_one = lax.psum_scatter(one_term, PLANE, scatter_dimension=0, tiled=True)
    weighted_one = weighted_one.astype(FULL)
    rank = lax.axis_index(ACROSS)
    out_part = out_sum.reshape(across, cols // across, width)
    out_part, *out_terms = [
        lax.dynamic_index_in_dim(out_part, (rank - step) % across, 0, keepdims=False)
        for step in range(across)
    ]
    qkv_received = to_others(qkv_terms, ACROSS)
    gate_up_received = [jnp.concatenate(parts, 0) for parts in zip(*gate_up_received)]
    gate_up_mine = added(gate_up_own, gate_up_received)
    qkv_own = rows_for(late_ones, qkv_grads, 0, 0, width // across, ACROSS)
    down_own = rows_for(late_hiddens, branch_rows, 0, 0, units)
    gate_up_blocks = swap_group(gate_up_mine.astype(LOW).reshape(group, -1, 2 * own_units))
    qkv_mine = added(qkv_own, qkv_received).astype(LOW)
    down_grad = added(
        down_own, [jnp.concatenate(parts, 0) for parts in zip(down_first, down_second)]
    )
    out_terms = after([term.astype(LOW) for term in out_terms], qkv_mine)
    out_grad = added(out_part, to_others(out_terms, ACROSS))
    if pieces != across:
        owners = [(z * plane + t, t * across + z) for z in range(across) for t in range(plane)]
        out_grad = lax.ppermute(out_grad.astype(LOW), EVERY, owners).astype(FULL)

    qkv_mine = after(qkv_mine.astype(LOW), gate_up_blocks)
    qkv_blocks = swap_group(qkv_mine.reshape(plane, -1, 3 * cols), PLANE)

    inverse_one = norm_scale(inputs)
    scaled_one = inputs * inverse_one
    input_grad = residual_grad + inverse_one * (
        weighted_one - scaled_one * jnp.mean(weighted_one * scaled_one, -1, keepdims=True)
    )
    gate_up_grad, gain_two_grad = collect(
        gate_up_blocks, gate_up_weight, gain_two, 2, w_size, units
    )
    qkv_grad, gain_one_grad = collect(qkv_blocks, qkv_weight, gain_one, 3, 1, cols, pieces)
    return (
        mixed[None],
        input_grad[None],
        gain_one_grad,
        qkv_grad,
        out_grad,
        gain_two_grad,
        gate_up_grad,
        down_grad,
    )


def solution(mesh):
    dp_size, _ = mesh.devices.shape
    fine = Mesh(mesh.devices.reshape(dp_size // 4, 2, 2, 2, 2), EVERY)
    token_spec = P(("w", "p", "q"), ("x", "c"), None)
    matrix, vector = P(EVERY, None), P(EVERY)
    return jax.shard_map(
        shards,
        mesh=fine,
        in_specs=(
            token_spec,
            P(("w", "p", "q"), None),
            vector,
            matrix,
            matrix,
            vector,
            matrix,
            matrix,
            token_spec,
        ),
        out_specs=(token_spec, token_spec, vector, matrix, matrix, vector, matrix, matrix),
        check_vma=False,
    )
```

```python
import functools
import math

import jax
import jax.numpy as jnp
from jax import lax
from jax.experimental import pallas as pl
from jax.experimental.pallas import tpu as pltpu
from jax.sharding import Mesh, PartitionSpec as P

HEAD_DIM = 64
EPSILON = 1e-05
ROPE_BASE = 130000.0
LANES = 128
LOW = jnp.bfloat16
FULL = jnp.float32
VMEM_BYTES = 50 * 1024 * 1024

CHUNK = 256

CUBE = ("p", "q", "x")
GROUP = ("p", "q", "x", "c")
PLANE = ("q", "x", "c")
ACROSS = ("w", "p")
EVERY = ("w", "p", "q", "x", "c")


def shift(value, axis, step):
    size = lax.axis_size(axis)
    if step % size == 0:
        return value
    return lax.ppermute(value, axis, [(i, (i + step) % size) for i in range(size)])


def flip(value, axis):
    return shift(value, axis, 1)


def together(*values):
    return lax.optimization_barrier(values)


def after(value, *earlier):
    return lax.optimization_barrier((value,) + earlier)[0]


def product(left, right):
    return jnp.dot(left, right, preferred_element_type=FULL)


def product_t(left, right):
    return lax.dot_general(left, right, (((1,), (1,)), ((), ())), preferred_element_type=FULL)


def t_product(left, right):
    return lax.dot_general(left, right, (((0,), (0,)), ((), ())), preferred_element_type=FULL)


SEQUENCES = ((), ("p",), ("q",), ("p", "q"))


def step(moves, flips, beside=()):
    values = together(*flips, *beside)
    try:
        later = moves.send(values[: len(flips)])
    except StopIteration as end:
        later = end.value
    return later, values[len(flips) :]


def pairs_of(parts, sequences):
    rows = parts[0].shape[0] // len(sequences)
    held = {}
    for index, along_x in enumerate(((), ("x",))):
        other = flip(parts[2 + index], "c")
        for row, place in enumerate(sequences):
            own = slice(row * rows, (row + 1) * rows)
            held[frozenset(place + along_x)] = parts[index][own].astype(FULL) + other[own].astype(
                FULL
            )
    return held


def scatter_steps(parts):
    held = pairs_of(parts, SEQUENCES)

    def send(key, axis):
        return flip(held[frozenset(key)].astype(LOW), axis)

    def add(key, *terms):
        for term in terms:
            held[frozenset(key)] = held[frozenset(key)] + term.astype(FULL)

    add("pq", *(yield [send("pqx", "x")]))
    one, two, three = yield [send("pq", "q"), send("qx", "x"), send("px", "p")]
    add("p", one)
    add("q", two)
    add("x", three)
    add("", *(yield [send("p", "p"), send("q", "q"), send("x", "x")]))
    return held[frozenset()]


def gather_plane(block):
    along_x, along_q, other = yield [flip(block, "x"), flip(block, "q"), flip(block, "c")]
    corner, other_x, other_q = yield [flip(along_x, "q"), flip(along_x, "c"), flip(along_q, "c")]
    (other_corner,) = yield [flip(corner, "c")]
    return [[block, along_x, other, other_x], [along_q, corner, other_q, other_corner]]


def scatter_plane(parts):
    held = pairs_of(parts, ((), ("q",)))
    own, along_x, along_q, corner = [held[frozenset(key)] for key in ("", "x", "q", "qx")]
    (term,) = yield [flip(corner.astype(LOW), "x")]
    along_q = along_q + term.astype(FULL)
    one, two = yield [flip(along_x.astype(LOW), "x"), flip(along_q.astype(LOW), "q")]
    return own + one.astype(FULL) + two.astype(FULL)


def swap_group(blocks, axes=GROUP):
    return lax.all_to_all(blocks, axes, 0, 0, tiled=True)


def from_others(block, axis="w"):
    return [shift(block, axis, step) for step in range(1, lax.axis_size(axis))]


def put(whole, start, blocks, axis="w"):
    size, rank = lax.axis_size(axis), lax.axis_index(axis)
    for step, block in enumerate(blocks):
        index = ((rank - step) % size, start) + (0,) * (block.ndim - 1)
        whole = lax.dynamic_update_slice(whole, block[None], index)
    return whole


def rows_for(left, right, step, low, high, axis="w"):
    size, rank = lax.axis_size(axis), lax.axis_index(axis)
    rows = left.shape[1] // size
    start = ((rank - step) % size) * rows + low
    return t_product(lax.dynamic_slice_in_dim(left, start, high - low, 1), right).astype(LOW)


def to_others(terms, axis="w"):
    return [shift(term, axis, -1 - index) for index, term in enumerate(terms)]


def terms_for(left, right, low, high, axis="w"):
    steps = range(1, lax.axis_size(axis))
    return [rows_for(left, right, step, low, high, axis) for step in steps]


def added(own, received):
    total = own.astype(FULL)
    for piece in received:
        total = total + piece.astype(FULL)
    return total


def spread_kernel(places, chunk, pieces, weight_ref, gain_ref, *refs):
    gain = gain_ref[...]
    out_ref = refs[-1]
    rows = weight_ref.shape[0]
    run = chunk // pieces
    for place in range(places):
        starts = [(piece * places + place) * run for piece in range(pieces)]
        parts = [weight_ref[:, start : start + run] for start in starts]
        part = parts[0] if pieces == 1 else jnp.concatenate(parts, 1)
        out_ref[place, :rows] = (part.astype(FULL) * gain).astype(LOW)
        for ref in refs[:-1]:
            out_ref[place, rows:] = ref[...]


def spread(weight, gain, places, outer, inner, chunk, pieces=1, more=()):
    rows, _ = weight.shape
    all_rows = rows + sum(array.shape[0] for array in more)
    count = outer * inner
    if chunk % LANES or (inner > 1 and chunk != CHUNK):
        scaled = (weight.astype(FULL) * gain).astype(LOW)
        if inner > 1:
            blocks = scaled.reshape(rows, outer, inner, places, chunk).transpose(3, 0, 1, 2, 4)
            blocks = blocks.reshape(places, rows, outer, inner * chunk // CHUNK, CHUNK)
            blocks = blocks.transpose(0, 1, 3, 2, 4)
        else:
            blocks = scaled.reshape(rows, outer, places, chunk).transpose(2, 0, 1, 3)
        return blocks.reshape(places, rows, count * chunk)
    return pl.pallas_call(
        functools.partial(spread_kernel, places, chunk, pieces),
        grid=(inner, outer),
        in_specs=[
            pl.BlockSpec((rows, places * chunk), lambda i, o: (0, o * inner + i)),
            pl.BlockSpec((rows, 1), lambda i, o: (0, 0)),
        ]
        + [pl.BlockSpec(array.shape, lambda i, o: (0, 0)) for array in more],
        out_specs=pl.BlockSpec((places, all_rows, chunk), lambda i, o: (0, 0, i * outer + o)),
        out_shape=jax.ShapeDtypeStruct((places, all_rows, count * chunk), LOW),
        compiler_params=pltpu.CompilerParams(vmem_limit_bytes=VMEM_BYTES),
    )(weight, gain, *more)


def collect_kernel(places, chunk, pieces, blocks_ref, weight_ref, gain_ref, grad_ref, total_ref):
    gain = gain_ref[...]

    @pl.when((pl.program_id(0) == 0) & (pl.program_id(1) == 0))
    def _():
        total_ref[...] = jnp.zeros_like(total_ref)

    total = total_ref[...]
    run = chunk // pieces
    step = max(1, LANES // run)
    for first in range(0, places, step):
        for piece in range(pieces):
            parts = [
                blocks_ref[place, :, piece * run : (piece + 1) * run].astype(FULL)
                for place in range(first, first + step)
            ]
            part = parts[0] if step == 1 else jnp.concatenate(parts, 1)
            start = (piece * places + first) * run
            end = start + step * run
            grad_ref[:, start:end] = part * gain
            terms = part * weight_ref[:, start:end].astype(FULL)
            for lane in range(0, step * run, LANES):
                total = total + terms[:, lane : lane + LANES]
    total_ref[...] = total


def collect(blocks, weight, gain, outer, inner, chunk, pieces=1):
    places, rows, _ = blocks.shape
    columns = weight.shape[1]
    if chunk % LANES or (inner > 1 and chunk != CHUNK):
        raw = blocks.astype(FULL)
        if inner > 1:
            raw = raw.reshape(places, rows, inner * chunk // CHUNK, outer, CHUNK)
            raw = raw.transpose(0, 1, 3, 2, 4)
        raw = raw.reshape(places, rows, outer, inner, chunk).transpose(1, 2, 3, 0, 4)
        raw = raw.reshape(rows, columns)
        return raw * gain, jnp.sum(raw * weight.astype(FULL), 1)
    grad, total = pl.pallas_call(
        functools.partial(collect_kernel, places, chunk, pieces),
        grid=(inner, outer),
        in_specs=[
            pl.BlockSpec((places, rows, chunk), lambda i, o: (0, 0, i * outer + o)),
            pl.BlockSpec((rows, places * chunk), lambda i, o: (0, o * inner + i)),
            pl.BlockSpec((rows, 1), lambda i, o: (0, 0)),
        ],
        out_specs=[
            pl.BlockSpec((rows, places * chunk), lambda i, o: (0, o * inner + i)),
            pl.BlockSpec((rows, LANES), lambda i, o: (0, 0)),
        ],
        out_shape=[
            jax.ShapeDtypeStruct((rows, columns), FULL),
            jax.ShapeDtypeStruct((rows, LANES), FULL),
        ],
        compiler_params=pltpu.CompilerParams(vmem_limit_bytes=VMEM_BYTES),
    )(blocks, weight, gain)
    return grad, jnp.sum(total, 1)


def rotate(values, cosines, sines, lower):
    half_dim = HEAD_DIM // 2
    width = values.shape[-1]
    other = jnp.where(
        lower, pltpu.roll(values, width - half_dim, 1), pltpu.roll(values, half_dim, 1)
    )
    return values * cosines + other * sines


def lower_half(shape):
    return lax.broadcasted_iota(jnp.int32, shape, 1) % HEAD_DIM < HEAD_DIM // 2


def head_lanes(shape, head):
    return lax.broadcasted_iota(jnp.int32, shape, 1) // HEAD_DIM == head


def allowed_pairs(seg_col, seg_row):
    length = seg_col.shape[0]
    shape = (length, length)
    earlier = lax.broadcasted_iota(jnp.int32, shape, 1) <= lax.broadcasted_iota(jnp.int32, shape, 0)
    return earlier & (seg_row[:1, :] == seg_col[...])


def rows_at(where, index, rows):
    return pl.ds(pl.multiple_of(where[where.shape[0] - 4 + index] * rows, rows), rows)


def store_parts(where, part_ref, part_refs):
    rows = part_refs[0].shape[0]
    for index, ref in enumerate(part_refs):
        ref[...] = part_ref[rows_at(where, index, rows), :].astype(LOW)


def attend_kernel(heads, where, *refs):
    tokens_ref, weight_ref, out_weight_ref, cos_ref, sin_ref, seg_col, seg_row = refs[:7]
    scaled_ref, qkv_ref, log_ref, out_ref = refs[7:11]
    part_refs, part_ref = refs[11:15], refs[15]
    cols = heads * HEAD_DIM
    block = tokens_ref[...].astype(FULL)
    mean = jnp.mean(block * block, -1, keepdims=True)
    scaled_ref[...] = (block * lax.rsqrt(mean + EPSILON)).astype(LOW)
    mixed = product(scaled_ref[...], weight_ref[...])
    cosines, sines = cos_ref[...], sin_ref[...]
    lower = lower_half(cosines.shape)
    query = rotate(mixed[:, :cols], cosines, sines, lower).astype(LOW)
    key = rotate(mixed[:, cols : 2 * cols], cosines, sines, lower).astype(LOW)
    value = mixed[:, 2 * cols :].astype(LOW)
    qkv_ref[:, :cols] = query
    qkv_ref[:, cols : 2 * cols] = key
    qkv_ref[:, 2 * cols :] = value
    allowed = allowed_pairs(seg_col, seg_row)
    logs = jnp.zeros(query.shape, FULL)
    attended = jnp.zeros(query.shape, FULL)
    for head in range(heads):
        own = head_lanes(query.shape, head)
        scores = product_t(jnp.where(own, query, 0), key) * HEAD_DIM**-0.5
        scores = jnp.where(allowed, scores, -1e30)
        highest = jnp.max(scores, -1, keepdims=True)
        expanded = jnp.exp(scores - highest)
        denominator = jnp.sum(expanded, -1, keepdims=True)
        probs_low = (expanded / denominator).astype(LOW)
        attended = jnp.where(own, product(probs_low, value), attended)
        logs = jnp.where(own, highest + jnp.log(denominator), logs)
    log_ref[...] = logs
    out_ref[...] = attended.astype(LOW)
    part_ref[...] = product(attended.astype(LOW), out_weight_ref[...])
    store_parts(where, part_ref, part_refs)


def attend_back_kernel(heads, where, *refs):
    blocks = refs[:8]
    qkv_ref, log_ref, out_ref, weight_ref, out_weight_ref = refs[8:13]
    cos_ref, sin_ref, seg_col, seg_row = refs[13:17]
    qkv_grad_ref, part_ref, sum_ref, block_ref = refs[17:]
    rows = blocks[0].shape[0]
    for turn in range(2):

        @pl.when(pl.program_id(0) == turn)
        def _():
            for index, ref in enumerate(blocks[4 * turn : 4 * turn + 4]):
                block_ref[rows_at(where, index, rows), :] = ref[...]

    term = t_product(out_ref[...], block_ref[...])

    @pl.when(pl.program_id(0) == 0)
    def _():
        sum_ref[...] = term

    @pl.when(pl.program_id(0) > 0)
    def _():
        sum_ref[...] += term

    cols = heads * HEAD_DIM
    query = qkv_ref[:, :cols]
    key = qkv_ref[:, cols : 2 * cols]
    value = qkv_ref[:, 2 * cols :]
    grad = product_t(block_ref[...], out_weight_ref[...]).astype(LOW)
    allowed = allowed_pairs(seg_col, seg_row)
    query_grad = jnp.zeros(query.shape, FULL)
    key_grad = jnp.zeros(query.shape, FULL)
    value_grad = jnp.zeros(query.shape, FULL)
    score_scale = HEAD_DIM**-0.5
    for head in range(heads):
        own = head_lanes(query.shape, head)
        scores = product_t(jnp.where(own, query, 0), key) * score_scale
        log_total = log_ref[:, head * HEAD_DIM : head * HEAD_DIM + 1]
        probs = jnp.where(allowed, jnp.exp(jnp.where(allowed, scores - log_total, 0.0)), 0.0)
        value_grad = jnp.where(own, t_product(probs.astype(LOW), grad), value_grad)
        prob_grad = product_t(jnp.where(own, grad, 0), value)
        row_terms = jnp.sum(probs * prob_grad, -1, keepdims=True)
        score_grad = (probs * (prob_grad - row_terms)).astype(LOW)
        query_grad = jnp.where(own, product(score_grad, key), query_grad)
        key_grad = jnp.where(own, t_product(score_grad, query), key_grad)
    cosines, sines = cos_ref[...], sin_ref[...]
    lower = lower_half(cosines.shape)
    query_low = rotate(query_grad * score_scale, cosines, -sines, lower).astype(LOW)
    key_low = rotate(key_grad * score_scale, cosines, -sines, lower).astype(LOW)
    value_low = value_grad.astype(LOW)
    qkv_grad_ref[:, :cols] = query_low
    qkv_grad_ref[:, cols : 2 * cols] = key_low
    qkv_grad_ref[:, 2 * cols :] = value_low
    part = product_t(query_low, weight_ref[:, :cols])
    part = part + product_t(key_low, weight_ref[:, cols : 2 * cols])
    part = part + product_t(value_low, weight_ref[:, 2 * cols :])
    part_ref[...] = part.astype(LOW)


def feed_kernel(where, *refs):
    scaled_ref, branch_ref, gate_up_ref, down_ref, hidden_ref, grad_ref = refs[:6]
    part_refs, part_ref = refs[6:10], refs[10]
    branch = branch_ref[...].reshape(scaled_ref.shape)
    for start in range(0, down_ref.shape[0], CHUNK):
        units = slice(start, start + CHUNK)
        both = slice(2 * start, 2 * start + 2 * CHUNK)
        gate_up = product(scaled_ref[...], gate_up_ref[:, both])
        gate, upper = gate_up[:, :CHUNK], gate_up[:, CHUNK:]
        sigmoid = 1.0 / (1.0 + jnp.exp(-gate))
        silu = gate * sigmoid
        hidden = (silu * upper).astype(LOW)
        hidden_ref[:, :, :, units] = hidden.reshape(*hidden_ref.shape[:3], CHUNK)
        hidden_grad = product_t(branch, down_ref[units, :])
        gate_grad = hidden_grad * upper * sigmoid * (1.0 + gate * (1.0 - sigmoid))
        grad_ref[:, 2 * start : 2 * start + CHUNK] = gate_grad.astype(LOW)
        grad_ref[:, 2 * start + CHUNK : 2 * start + 2 * CHUNK] = (hidden_grad * silu).astype(LOW)
    part_ref[...] = product_t(grad_ref[...], gate_up_ref[...])
    store_parts(where, part_ref, part_refs)


def on_sequences(kernel, where, operands, results, scratch, flops, exps):
    def spec(shape, rows):
        if isinstance(rows, tuple):
            return pl.BlockSpec(*rows)
        if rows > 0:
            return pl.BlockSpec((rows, *shape[1:]), lambda i, where: (where[i], 0))
        if rows < 0:
            return pl.BlockSpec((-rows, *shape[1:]), lambda i, where: (i, 0))
        return pl.BlockSpec(shape, lambda i, where: (0, 0))

    moved = sum(array.size * array.dtype.itemsize for array, _ in operands) // 16
    flops, exps = flops // 16, exps // 16
    return pl.pallas_call(
        kernel,
        grid_spec=pltpu.PrefetchScalarGridSpec(
            num_scalar_prefetch=1,
            grid=(where.shape[0] - 4,),
            in_specs=[spec(array.shape, rows) for array, rows in operands],
            out_specs=[spec(shape, rows) for (shape, _), rows in results],
            scratch_shapes=scratch,
        ),
        out_shape=[jax.ShapeDtypeStruct(shape, dtype) for (shape, dtype), _ in results],
        compiler_params=pltpu.CompilerParams(vmem_limit_bytes=VMEM_BYTES),
        cost_estimate=pl.CostEstimate(flops=flops, bytes_accessed=moved, transcendentals=exps),
    )(where, *[array for array, _ in operands])


def shards(
    tokens,
    segment_ids,
    gain_first,
    qkv_weight,
    out_weight,
    gain_second,
    gate_up_weight,
    down_weight,
    cotangent,
):
    w_size = lax.axis_size("w")
    group = 16
    p_rank, q_rank, x_rank, c_rank = (lax.axis_index(axis) for axis in GROUP)
    own_tokens = tokens[0]
    rows, width = own_tokens.shape
    length = 4 * rows
    group_rows = 4 * length
    units = down_weight.shape[0]
    own_units = w_size * units
    plane, across = 8, 2 * w_size
    plane_rows = 2 * length
    cols = width // plane
    heads = cols // HEAD_DIM

    places = [(x_rank ^ jx) * 2 + (c_rank ^ jc) for jc in range(2) for jx in range(2)]
    wheres = [(p_rank ^ jp) * 2 + (q_rank ^ jq) for jp, jq in ((0, 0), (1, 0), (0, 1), (1, 1))]
    wheres = jnp.stack(wheres + places).astype(jnp.int32)
    cube_spec = ((4, 1, rows, width), lambda i, where: (where[i] % 2, i % 2, 0, 0))
    unit_spec = ((4, 1, rows, own_units), cube_spec[1])
    plane_wheres = jnp.stack([q_rank, q_rank ^ 1] + places).astype(jnp.int32)
    pieces = across if out_weight.shape[0] == HEAD_DIM else 1
    own_segments = segment_ids[0].astype(LOW).reshape(-1, cols)
    own_segments = jnp.pad(own_segments, ((0, -own_segments.shape[0] % 16), (0, 0)))
    half_dim = HEAD_DIM // 2
    freqs = jnp.exp(jnp.arange(half_dim).astype(FULL) * (-2.0 * math.log(ROPE_BASE) / HEAD_DIM))
    angles = jnp.arange(length).astype(FULL)[:, None] * freqs[None, :]
    cosines = jnp.tile(jnp.cos(angles), (1, 2 * heads))
    sines = jnp.tile(jnp.concatenate([-jnp.sin(angles), jnp.sin(angles)], 1), (1, heads))

    gain_one = gain_first.astype(FULL)[:, None]
    gain_two = gain_second.astype(FULL)[:, None]
    count = w_size - 1
    qkv_blocks = spread(qkv_weight, gain_one, plane, 3, 1, cols, pieces, [own_segments])

    tokens_all = lax.all_gather(own_tokens, PLANE, axis=0, tiled=True)
    out_received = from_others(out_weight, ACROSS) if pieces == across else []
    qkv_blocks, branch_pair, gate_up_own, *out_received = together(
        swap_group(qkv_blocks, PLANE),
        flip(cotangent[0], "p"),
        spread(gate_up_weight, gain_two, group, 2, w_size, units),
        *out_received,
    )
    if pieces == across:
        out_rows = jnp.zeros((across, *out_weight.shape), LOW)
        out_rows = put(out_rows, 0, [out_weight, *out_received], ACROSS).reshape(cols, width)
    else:
        out_rows = lax.all_gather(out_weight, EVERY, axis=0, tiled=True)
        out_rows = lax.dynamic_slice_in_dim(out_rows, lax.axis_index(PLANE) * cols, cols)
    qkv_own = qkv_blocks[:, : qkv_weight.shape[0]].reshape(-1, 3 * cols)
    all_segments = qkv_blocks[::4, qkv_weight.shape[0] :].reshape(2, -1)
    all_segments = all_segments.reshape(2, -1, 3, cols)[:, :, 0].reshape(2, -1)
    all_segments = all_segments[:, :length].astype(jnp.int32)
    branch_all = lax.all_gather(jnp.stack([cotangent[0], branch_pair]), PLANE)
    gate_up_own = swap_group(gate_up_own)
    weight_rows = group * gate_up_weight.shape[0]
    gate_up_own = gate_up_own.reshape(weight_rows, 2 * own_units)
    qkv_received = from_others(qkv_own, ACROSS)
    qkv_cols = jnp.zeros((across, *qkv_own.shape), LOW)
    qkv_cols = put(qkv_cols, 0, [qkv_own, *qkv_received], ACROSS).reshape(width, 3 * cols)
    ends = [0, weight_rows // 2, weight_rows]
    gate_up_parts = [gate_up_own[low:high] for low, high in zip(ends, ends[1:])]
    gate_up_cols = jnp.zeros((w_size, weight_rows, 2 * own_units), LOW)

    seg_col = all_segments.reshape(plane_rows, 1)
    seg_row = jnp.broadcast_to(all_segments[:, None], (2, 8, length)).reshape(16, length)
    scaled_ones, qkv_lows, logs, attended_heads, *out_parts = on_sequences(
        functools.partial(attend_kernel, heads),
        plane_wheres,
        [
            (tokens_all, length),
            (qkv_cols, 0),
            (out_rows, 0),
            (cosines, 0),
            (sines, 0),
            (seg_col, length),
            (seg_row, 8),
        ],
        [
            (((plane_rows, width), LOW), length),
            (((plane_rows, 3 * cols), LOW), length),
            (((plane_rows, cols), FULL), length),
            (((plane_rows, cols), LOW), length),
        ]
        + [(((2 * rows, width), LOW), -rows)] * 4,
        [pltpu.VMEM((length, width), FULL)],
        4 * length * width * 4 * cols + 8 * heads * length * length * LANES,
        2 * heads * length * length,
    )

    def norm_scale(values):
        return lax.rsqrt(jnp.mean(values * values, -1, keepdims=True) + EPSILON)

    def put_gate_up(whole, index, received):
        return put(whole, ends[index], [gate_up_parts[index], *received])

    moves = scatter_plane(out_parts)
    down_others = from_others(after(down_weight, *qkv_received))
    flips, _ = step(moves, next(moves))
    out_sum, (down_others, gate_up_parts) = step(moves, flips, [down_others, gate_up_parts])
    inputs = own_tokens.astype(FULL)
    residual = inputs + out_sum
    inverse_two = norm_scale(residual)
    scaled_two = residual * inverse_two
    scaled_twos = lax.all_gather(scaled_two.astype(LOW), GROUP, axis=0, tiled=True)
    received = down_others
    for index in range(2):
        received = from_others(after(gate_up_parts[index], *received))
        gate_up_cols = put_gate_up(gate_up_cols, index, received)
    gate_up_cols = gate_up_cols.reshape(width, 2 * own_units)
    down_rows = jnp.zeros((w_size, units, width), LOW)
    down_rows = put(down_rows, 0, [down_weight, *down_others]).reshape(own_units, width)

    unit_rows, gate_up_grads, *two_parts = on_sequences(
        feed_kernel,
        wheres,
        [(scaled_twos, length), (branch_all, cube_spec), (gate_up_cols, 0), (down_rows, 0)],
        [
            (((plane, 2, rows, own_units), LOW), unit_spec),
            (((group_rows, 2 * own_units), LOW), length),
        ]
        + [(((4 * rows, width), LOW), -rows)] * 4,
        [pltpu.VMEM((length, width), FULL)],
        40 * length * width * own_units,
        4 * length * own_units,
    )

    hiddens = unit_rows.reshape(group_rows, own_units)
    branch_rows = branch_all.reshape(group_rows, width)

    def gate_up_terms(left, index):
        return terms_for(left, gate_up_grads, ends[index], ends[index + 1])

    moves = scatter_steps(two_parts)
    down_terms = terms_for(hiddens, branch_rows, 0, units)
    late_scaled = after(scaled_twos, *down_terms)
    terms = [gate_up_terms(late_scaled, index) for index in range(2)]
    down_sent = [
        [term[: units // 2] for term in down_terms],
        [term[units // 2 :] for term in down_terms],
    ]
    flips, (terms, down_first) = step(moves, next(moves), [terms, to_others(down_sent[0])])
    mixed_term = product(after(hiddens, flips), down_rows).astype(LOW)
    down_second = to_others(after(down_sent[1], *down_first))
    flips, (down_second, mixed_term) = step(moves, flips, [down_second, mixed_term])
    down_received = [jnp.concatenate(parts, 0) for parts in zip(down_first, down_second)]
    mixed_sum = lax.psum_scatter(mixed_term, PLANE, scatter_dimension=0, tiled=True)
    gate_up_own = rows_for(after(scaled_twos, flips), gate_up_grads, 0, 0, weight_rows)
    weighted_two, (gate_up_own,) = step(moves, flips, [gate_up_own])
    upstream = cotangent[0].astype(FULL)
    residual_grad = upstream + inverse_two * (
        weighted_two - scaled_two * jnp.mean(weighted_two * scaled_two, -1, keepdims=True)
    )
    attn_grad_low = residual_grad.astype(LOW)
    moves = gather_plane(attn_grad_low)
    first_rows = to_others(after(terms[0], *down_second))
    flips, (first_rows,) = step(moves, next(moves), [first_rows])
    flips, _ = step(moves, flips)
    second_rows = to_others(after(terms[1], *first_rows))
    grad_blocks, _ = step(moves, flips)
    qkv_grads, one_term, out_sum = on_sequences(
        functools.partial(attend_back_kernel, heads),
        plane_wheres,
        [(block, 0) for blocks in grad_blocks for block in blocks]
        + [(qkv_lows, length), (logs, length), (attended_heads, length)]
        + [(array, 0) for array in (qkv_cols, out_rows, cosines, sines)]
        + [(seg_col, length), (seg_row, 8)],
        [
            (((plane_rows, 3 * cols), LOW), length),
            (((plane_rows, width), LOW), length),
            (((cols, width), FULL), 0),
        ],
        [pltpu.VMEM((length, width), LOW)],
        4 * length * width * 5 * cols + 20 * heads * length * length * LANES,
        2 * heads * length * length,
    )
    qkv_grads, one_term, out_sum, second_rows = together(
        qkv_grads, one_term, out_sum, second_rows
    )
    gate_up_received = [first_rows, second_rows]
    mixed_rows = after(mixed_sum, qkv_grads)
    mixed_sum = added(mixed_rows[:rows], [flip(mixed_rows[rows:], "p")])
    mixed = (residual + mixed_sum).astype(LOW)
    late_ones = after(scaled_ones, qkv_grads)
    qkv_terms = terms_for(late_ones, qkv_grads, 0, width // across, ACROSS)
    late_hiddens = after(hiddens, *qkv_terms)
    one_term = after(one_term, mixed_rows)
    weighted_one = lax.psum_scatter(one_term, PLANE, scatter_dimension=0, tiled=True)
    weighted_one = weighted_one.astype(FULL)
    rank = lax.axis_index(ACROSS)
    out_part = out_sum.reshape(across, cols // across, width)
    out_part, *out_terms = [
        lax.dynamic_index_in_dim(out_part, (rank - step) % across, 0, keepdims=False)
        for step in range(across)
    ]
    qkv_received = to_others(qkv_terms, ACROSS)
    gate_up_received = [jnp.concatenate(parts, 0) for parts in zip(*gate_up_received)]
    gate_up_mine = added(gate_up_own, gate_up_received)
    qkv_own = rows_for(late_ones, qkv_grads, 0, 0, width // across, ACROSS)
    down_own = rows_for(late_hiddens, branch_rows, 0, 0, units)
    gate_up_blocks = swap_group(gate_up_mine.astype(LOW).reshape(group, -1, 2 * own_units))
    qkv_mine = added(qkv_own, qkv_received).astype(LOW)
    down_grad = added(
        down_own, down_received
    )
    out_terms = after([term.astype(LOW) for term in out_terms], qkv_mine)
    out_grad = added(out_part, to_others(out_terms, ACROSS))
    if pieces != across:
        owners = [(z * plane + t, t * across + z) for z in range(across) for t in range(plane)]
        out_grad = lax.ppermute(out_grad.astype(LOW), EVERY, owners).astype(FULL)

    qkv_mine = after(qkv_mine.astype(LOW), gate_up_blocks)
    qkv_blocks = swap_group(qkv_mine.reshape(plane, -1, 3 * cols), PLANE)

    inverse_one = norm_scale(inputs)
    scaled_one = inputs * inverse_one
    input_grad = residual_grad + inverse_one * (
        weighted_one - scaled_one * jnp.mean(weighted_one * scaled_one, -1, keepdims=True)
    )
    gate_up_grad, gain_two_grad = collect(
        gate_up_blocks, gate_up_weight, gain_two, 2, w_size, units
    )
    qkv_grad, gain_one_grad = collect(qkv_blocks, qkv_weight, gain_one, 3, 1, cols, pieces)
    return (
        mixed[None],
        input_grad[None],
        gain_one_grad,
        qkv_grad,
        out_grad,
        gain_two_grad,
        gate_up_grad,
        down_grad,
    )


def solution(mesh):
    dp_size, _ = mesh.devices.shape
    fine = Mesh(mesh.devices.reshape(dp_size // 4, 2, 2, 2, 2), EVERY)
    token_spec = P(("w", "p", "q"), ("x", "c"), None)
    matrix, vector = P(EVERY, None), P(EVERY)
    return jax.shard_map(
        shards,
        mesh=fine,
        in_specs=(
            token_spec,
            P(("w", "p", "q"), None),
            vector,
            matrix,
            matrix,
            vector,
            matrix,
            matrix,
            token_spec,
        ),
        out_specs=(token_spec, token_spec, vector, matrix, matrix, vector, matrix, matrix),
        check_vma=False,
    )
```

```python
import functools
import math

import jax
import jax.numpy as jnp
from jax import lax
from jax.experimental import pallas as pl
from jax.experimental.pallas import tpu as pltpu
from jax.sharding import Mesh, PartitionSpec as P

HEAD_DIM = 64
EPSILON = 1e-05
ROPE_BASE = 130000.0
LANES = 128
LOW = jnp.bfloat16
FULL = jnp.float32
VMEM_BYTES = 50 * 1024 * 1024

CHUNK = 256

CUBE = ("p", "q", "x")
GROUP = ("p", "q", "x", "c")
PLANE = ("q", "x", "c")
ACROSS = ("w", "p")
EVERY = ("w", "p", "q", "x", "c")


def shift(value, axis, step):
    size = lax.axis_size(axis)
    if step % size == 0:
        return value
    return lax.ppermute(value, axis, [(i, (i + step) % size) for i in range(size)])


def flip(value, axis):
    return shift(value, axis, 1)


def together(*values):
    return lax.optimization_barrier(values)


def after(value, *earlier):
    return lax.optimization_barrier((value,) + earlier)[0]


def product(left, right):
    return jnp.dot(left, right, preferred_element_type=FULL)


def product_t(left, right):
    return lax.dot_general(left, right, (((1,), (1,)), ((), ())), preferred_element_type=FULL)


def t_product(left, right):
    return lax.dot_general(left, right, (((0,), (0,)), ((), ())), preferred_element_type=FULL)


SEQUENCES = ((), ("p",), ("q",), ("p", "q"))


def step(moves, flips, beside=()):
    values = together(*flips, *beside)
    try:
        later = moves.send(values[: len(flips)])
    except StopIteration as end:
        later = end.value
    return later, values[len(flips) :]


def pairs_of(parts, sequences):
    rows = parts[0].shape[0] // len(sequences)
    held = {}
    for index, along_x in enumerate(((), ("x",))):
        other = flip(parts[2 + index], "c")
        for row, place in enumerate(sequences):
            own = slice(row * rows, (row + 1) * rows)
            held[frozenset(place + along_x)] = parts[index][own].astype(FULL) + other[own].astype(
                FULL
            )
    return held


def scatter_steps(parts):
    held = pairs_of(parts, SEQUENCES)

    def send(key, axis):
        return flip(held[frozenset(key)].astype(LOW), axis)

    def add(key, *terms):
        for term in terms:
            held[frozenset(key)] = held[frozenset(key)] + term.astype(FULL)

    add("pq", *(yield [send("pqx", "x")]))
    one, two, three = yield [send("pq", "q"), send("qx", "x"), send("px", "p")]
    add("p", one)
    add("q", two)
    add("x", three)
    add("", *(yield [send("p", "p"), send("q", "q"), send("x", "x")]))
    return held[frozenset()]


def scatter_plane(parts):
    held = pairs_of(parts, ((), ("q",)))
    own, along_x, along_q, corner = [held[frozenset(key)] for key in ("", "x", "q", "qx")]
    (term,) = yield [flip(corner.astype(LOW), "x")]
    along_q = along_q + term.astype(FULL)
    one, two = yield [flip(along_x.astype(LOW), "x"), flip(along_q.astype(LOW), "q")]
    return own + one.astype(FULL) + two.astype(FULL)


def swap_group(blocks, axes=GROUP):
    return lax.all_to_all(blocks, axes, 0, 0, tiled=True)


def from_others(block, axis="w"):
    return [shift(block, axis, step) for step in range(1, lax.axis_size(axis))]


def put(whole, start, blocks, axis="w"):
    size, rank = lax.axis_size(axis), lax.axis_index(axis)
    for step, block in enumerate(blocks):
        index = ((rank - step) % size, start) + (0,) * (block.ndim - 1)
        whole = lax.dynamic_update_slice(whole, block[None], index)
    return whole


def rows_for(left, right, step, low, high, axis="w"):
    size, rank = lax.axis_size(axis), lax.axis_index(axis)
    rows = left.shape[1] // size
    start = ((rank - step) % size) * rows + low
    return t_product(lax.dynamic_slice_in_dim(left, start, high - low, 1), right).astype(LOW)


def to_others(terms, axis="w"):
    return [shift(term, axis, -1 - index) for index, term in enumerate(terms)]


def terms_for(left, right, low, high, axis="w"):
    steps = range(1, lax.axis_size(axis))
    return [rows_for(left, right, step, low, high, axis) for step in steps]


def added(own, received):
    total = own.astype(FULL)
    for piece in received:
        total = total + piece.astype(FULL)
    return total


def spread_kernel(places, chunk, pieces, weight_ref, gain_ref, *refs):
    gain = gain_ref[...]
    out_ref = refs[-1]
    rows = weight_ref.shape[0]
    run = chunk // pieces
    for place in range(places):
        starts = [(piece * places + place) * run for piece in range(pieces)]
        parts = [weight_ref[:, start : start + run] for start in starts]
        part = parts[0] if pieces == 1 else jnp.concatenate(parts, 1)
        out_ref[place, :rows] = (part.astype(FULL) * gain).astype(LOW)
        for ref in refs[:-1]:
            out_ref[place, rows:] = ref[...]


def spread(weight, gain, places, outer, inner, chunk, pieces=1, more=()):
    rows, _ = weight.shape
    all_rows = rows + sum(array.shape[0] for array in more)
    count = outer * inner
    if chunk % LANES or (inner > 1 and chunk != CHUNK):
        scaled = (weight.astype(FULL) * gain).astype(LOW)
        if inner > 1:
            blocks = scaled.reshape(rows, outer, inner, places, chunk).transpose(3, 0, 1, 2, 4)
            blocks = blocks.reshape(places, rows, outer, inner * chunk // CHUNK, CHUNK)
            blocks = blocks.transpose(0, 1, 3, 2, 4)
        else:
            blocks = scaled.reshape(rows, outer, places, chunk).transpose(2, 0, 1, 3)
        return blocks.reshape(places, rows, count * chunk)
    return pl.pallas_call(
        functools.partial(spread_kernel, places, chunk, pieces),
        grid=(inner, outer),
        in_specs=[
            pl.BlockSpec((rows, places * chunk), lambda i, o: (0, o * inner + i)),
            pl.BlockSpec((rows, 1), lambda i, o: (0, 0)),
        ]
        + [pl.BlockSpec(array.shape, lambda i, o: (0, 0)) for array in more],
        out_specs=pl.BlockSpec((places, all_rows, chunk), lambda i, o: (0, 0, i * outer + o)),
        out_shape=jax.ShapeDtypeStruct((places, all_rows, count * chunk), LOW),
        compiler_params=pltpu.CompilerParams(vmem_limit_bytes=VMEM_BYTES),
    )(weight, gain, *more)


def collect_kernel(places, chunk, pieces, blocks_ref, weight_ref, gain_ref, grad_ref, total_ref):
    gain = gain_ref[...]

    @pl.when((pl.program_id(0) == 0) & (pl.program_id(1) == 0))
    def _():
        total_ref[...] = jnp.zeros_like(total_ref)

    total = total_ref[...]
    run = chunk // pieces
    step = max(1, LANES // run)
    for first in range(0, places, step):
        for piece in range(pieces):
            parts = [
                blocks_ref[place, :, piece * run : (piece + 1) * run].astype(FULL)
                for place in range(first, first + step)
            ]
            part = parts[0] if step == 1 else jnp.concatenate(parts, 1)
            start = (piece * places + first) * run
            end = start + step * run
            grad_ref[:, start:end] = part * gain
            terms = part * weight_ref[:, start:end].astype(FULL)
            for lane in range(0, step * run, LANES):
                total = total + terms[:, lane : lane + LANES]
    total_ref[...] = total


def collect(blocks, weight, gain, outer, inner, chunk, pieces=1):
    places, rows, _ = blocks.shape
    columns = weight.shape[1]
    if chunk % LANES or (inner > 1 and chunk != CHUNK):
        raw = blocks.astype(FULL)
        if inner > 1:
            raw = raw.reshape(places, rows, inner * chunk // CHUNK, outer, CHUNK)
            raw = raw.transpose(0, 1, 3, 2, 4)
        raw = raw.reshape(places, rows, outer, inner, chunk).transpose(1, 2, 3, 0, 4)
        raw = raw.reshape(rows, columns)
        return raw * gain, jnp.sum(raw * weight.astype(FULL), 1)
    grad, total = pl.pallas_call(
        functools.partial(collect_kernel, places, chunk, pieces),
        grid=(inner, outer),
        in_specs=[
            pl.BlockSpec((places, rows, chunk), lambda i, o: (0, 0, i * outer + o)),
            pl.BlockSpec((rows, places * chunk), lambda i, o: (0, o * inner + i)),
            pl.BlockSpec((rows, 1), lambda i, o: (0, 0)),
        ],
        out_specs=[
            pl.BlockSpec((rows, places * chunk), lambda i, o: (0, o * inner + i)),
            pl.BlockSpec((rows, LANES), lambda i, o: (0, 0)),
        ],
        out_shape=[
            jax.ShapeDtypeStruct((rows, columns), FULL),
            jax.ShapeDtypeStruct((rows, LANES), FULL),
        ],
        compiler_params=pltpu.CompilerParams(vmem_limit_bytes=VMEM_BYTES),
    )(blocks, weight, gain)
    return grad, jnp.sum(total, 1)


def rotate(values, cosines, sines, lower):
    half_dim = HEAD_DIM // 2
    width = values.shape[-1]
    other = jnp.where(
        lower, pltpu.roll(values, width - half_dim, 1), pltpu.roll(values, half_dim, 1)
    )
    return values * cosines + other * sines


def lower_half(shape):
    return lax.broadcasted_iota(jnp.int32, shape, 1) % HEAD_DIM < HEAD_DIM // 2


def head_lanes(shape, head):
    return lax.broadcasted_iota(jnp.int32, shape, 1) // HEAD_DIM == head


def allowed_pairs(seg_col, seg_row):
    length = seg_col.shape[0]
    shape = (length, length)
    earlier = lax.broadcasted_iota(jnp.int32, shape, 1) <= lax.broadcasted_iota(jnp.int32, shape, 0)
    return earlier & (seg_row[:1, :] == seg_col[...])


def rows_at(where, index, rows):
    return pl.ds(pl.multiple_of(where[where.shape[0] - 4 + index] * rows, rows), rows)


def store_parts(where, part_ref, part_refs):
    rows = part_refs[0].shape[0]
    for index, ref in enumerate(part_refs):
        ref[...] = part_ref[rows_at(where, index, rows), :].astype(LOW)


def attend_kernel(heads, where, *refs):
    tokens_ref, weight_ref, out_weight_ref, cos_ref, sin_ref, seg_col, seg_row = refs[:7]
    scaled_ref, qkv_ref, log_ref, out_ref = refs[7:11]
    part_refs, part_ref = refs[11:15], refs[15]
    cols = heads * HEAD_DIM
    block = tokens_ref[...].astype(FULL)
    mean = jnp.mean(block * block, -1, keepdims=True)
    scaled_ref[...] = (block * lax.rsqrt(mean + EPSILON)).astype(LOW)
    mixed = product(scaled_ref[...], weight_ref[...])
    cosines, sines = cos_ref[...], sin_ref[...]
    lower = lower_half(cosines.shape)
    query = rotate(mixed[:, :cols], cosines, sines, lower).astype(LOW)
    key = rotate(mixed[:, cols : 2 * cols], cosines, sines, lower).astype(LOW)
    value = mixed[:, 2 * cols :].astype(LOW)
    qkv_ref[:, :cols] = query
    qkv_ref[:, cols : 2 * cols] = key
    qkv_ref[:, 2 * cols :] = value
    allowed = allowed_pairs(seg_col, seg_row)
    logs = jnp.zeros(query.shape, FULL)
    attended = jnp.zeros(query.shape, FULL)
    for head in range(heads):
        own = head_lanes(query.shape, head)
        scores = product_t(jnp.where(own, query, 0), key) * HEAD_DIM**-0.5
        scores = jnp.where(allowed, scores, -1e30)
        highest = jnp.max(scores, -1, keepdims=True)
        expanded = jnp.exp(scores - highest)
        denominator = jnp.sum(expanded, -1, keepdims=True)
        probs_low = (expanded / denominator).astype(LOW)
        attended = jnp.where(own, product(probs_low, value), attended)
        logs = jnp.where(own, highest + jnp.log(denominator), logs)
    log_ref[...] = logs
    out_ref[...] = attended.astype(LOW)
    part_ref[...] = product(attended.astype(LOW), out_weight_ref[...])
    store_parts(where, part_ref, part_refs)


def attend_back_kernel(heads, where, *refs):
    blocks = refs[:4]
    qkv_ref, log_ref, out_ref, before_ref, weight_ref, out_weight_ref = refs[4:10]
    cos_ref, sin_ref, seg_col, seg_row = refs[10:14]
    qkv_grad_ref, part_ref, sum_ref, block_ref = refs[-4:]
    rows = blocks[0].shape[0]
    for index, ref in enumerate(blocks):
        block_ref[rows_at(where, index, rows), :] = ref[...]
    sum_ref[...] = before_ref[...] + t_product(out_ref[...], block_ref[...])
    cols = heads * HEAD_DIM
    query = qkv_ref[:, :cols]
    key = qkv_ref[:, cols : 2 * cols]
    value = qkv_ref[:, 2 * cols :]
    grad = product_t(block_ref[...], out_weight_ref[...]).astype(LOW)
    allowed = allowed_pairs(seg_col, seg_row)
    query_grad = jnp.zeros(query.shape, FULL)
    key_grad = jnp.zeros(query.shape, FULL)
    value_grad = jnp.zeros(query.shape, FULL)
    score_scale = HEAD_DIM**-0.5
    for head in range(heads):
        own = head_lanes(query.shape, head)
        scores = product_t(jnp.where(own, query, 0), key) * score_scale
        log_total = log_ref[:, head * HEAD_DIM : head * HEAD_DIM + 1]
        probs = jnp.where(allowed, jnp.exp(jnp.where(allowed, scores - log_total, 0.0)), 0.0)
        value_grad = jnp.where(own, t_product(probs.astype(LOW), grad), value_grad)
        prob_grad = product_t(jnp.where(own, grad, 0), value)
        row_terms = jnp.sum(probs * prob_grad, -1, keepdims=True)
        score_grad = (probs * (prob_grad - row_terms)).astype(LOW)
        query_grad = jnp.where(own, product(score_grad, key), query_grad)
        key_grad = jnp.where(own, t_product(score_grad, query), key_grad)
    cosines, sines = cos_ref[...], sin_ref[...]
    lower = lower_half(cosines.shape)
    query_low = rotate(query_grad * score_scale, cosines, -sines, lower).astype(LOW)
    key_low = rotate(key_grad * score_scale, cosines, -sines, lower).astype(LOW)
    value_low = value_grad.astype(LOW)
    qkv_grad_ref[:, :cols] = query_low
    qkv_grad_ref[:, cols : 2 * cols] = key_low
    qkv_grad_ref[:, 2 * cols :] = value_low
    part = product_t(query_low, weight_ref[:, :cols])
    part = part + product_t(key_low, weight_ref[:, cols : 2 * cols])
    part = part + product_t(value_low, weight_ref[:, 2 * cols :])
    part_ref[...] = part.astype(LOW)


def feed_kernel(where, *refs):
    scaled_ref, branch_ref, gate_up_ref, down_ref, hidden_ref, grad_ref = refs[:6]
    part_refs, part_ref = refs[6:10], refs[10]
    branch = branch_ref[...].reshape(scaled_ref.shape)
    for start in range(0, down_ref.shape[0], CHUNK):
        units = slice(start, start + CHUNK)
        both = slice(2 * start, 2 * start + 2 * CHUNK)
        gate_up = product(scaled_ref[...], gate_up_ref[:, both])
        gate, upper = gate_up[:, :CHUNK], gate_up[:, CHUNK:]
        sigmoid = 1.0 / (1.0 + jnp.exp(-gate))
        silu = gate * sigmoid
        hidden = (silu * upper).astype(LOW)
        hidden_ref[:, :, :, units] = hidden.reshape(*hidden_ref.shape[:3], CHUNK)
        hidden_grad = product_t(branch, down_ref[units, :])
        gate_grad = hidden_grad * upper * sigmoid * (1.0 + gate * (1.0 - sigmoid))
        grad_ref[:, 2 * start : 2 * start + CHUNK] = gate_grad.astype(LOW)
        grad_ref[:, 2 * start + CHUNK : 2 * start + 2 * CHUNK] = (hidden_grad * silu).astype(LOW)
    part_ref[...] = product_t(grad_ref[...], gate_up_ref[...])
    store_parts(where, part_ref, part_refs)


def on_sequences(kernel, where, operands, results, scratch, flops, exps, held=()):
    def spec(shape, rows):
        if isinstance(rows, tuple):
            return pl.BlockSpec(*rows)
        if rows > 0:
            return pl.BlockSpec((rows, *shape[1:]), lambda i, where: (where[i], 0))
        if rows < 0:
            return pl.BlockSpec((-rows, *shape[1:]), lambda i, where: (i, 0))
        return pl.BlockSpec(shape, lambda i, where: (0, 0))

    moved = sum(array.size * array.dtype.itemsize for array, _ in operands) // 16
    flops, exps = flops // 16, exps // 16
    return pl.pallas_call(
        kernel,
        grid_spec=pltpu.PrefetchScalarGridSpec(
            num_scalar_prefetch=1,
            grid=(where.shape[0] - 4,),
            in_specs=[spec(array.shape, rows) for array, rows in operands]
            + [pl.BlockSpec(memory_space=pl.ANY) for _ in held],
            out_specs=[spec(shape, rows) for (shape, _), rows in results],
            scratch_shapes=scratch,
        ),
        out_shape=[jax.ShapeDtypeStruct(shape, dtype) for (shape, dtype), _ in results],
        input_output_aliases={1 + len(operands) + i: i for i in range(len(held))},
        compiler_params=pltpu.CompilerParams(vmem_limit_bytes=VMEM_BYTES),
        cost_estimate=pl.CostEstimate(flops=flops, bytes_accessed=moved, transcendentals=exps),
    )(where, *[array for array, _ in operands], *held)


def shards(
    tokens,
    segment_ids,
    gain_first,
    qkv_weight,
    out_weight,
    gain_second,
    gate_up_weight,
    down_weight,
    cotangent,
):
    w_size = lax.axis_size("w")
    group = 16
    p_rank, q_rank, x_rank, c_rank = (lax.axis_index(axis) for axis in GROUP)
    own_tokens = tokens[0]
    rows, width = own_tokens.shape
    length = 4 * rows
    group_rows = 4 * length
    units = down_weight.shape[0]
    own_units = w_size * units
    plane, across = 8, 2 * w_size
    plane_rows = 2 * length
    cols = width // plane
    heads = cols // HEAD_DIM

    places = [(x_rank ^ jx) * 2 + (c_rank ^ jc) for jc in range(2) for jx in range(2)]
    wheres = [(p_rank ^ jp) * 2 + (q_rank ^ jq) for jp, jq in ((0, 0), (1, 0), (0, 1), (1, 1))]
    wheres = jnp.stack(wheres + places).astype(jnp.int32)
    cube_spec = ((4, 1, rows, width), lambda i, where: (where[i] % 2, i % 2, 0, 0))
    unit_spec = ((4, 1, rows, own_units), cube_spec[1])
    plane_wheres = jnp.stack([q_rank, q_rank ^ 1] + places).astype(jnp.int32)
    pieces = across if out_weight.shape[0] == HEAD_DIM else 1
    own_segments = segment_ids[0].astype(LOW).reshape(-1, cols)
    own_segments = jnp.pad(own_segments, ((0, -own_segments.shape[0] % 16), (0, 0)))
    half_dim = HEAD_DIM // 2
    freqs = jnp.exp(jnp.arange(half_dim).astype(FULL) * (-2.0 * math.log(ROPE_BASE) / HEAD_DIM))
    angles = jnp.arange(length).astype(FULL)[:, None] * freqs[None, :]
    cosines = jnp.tile(jnp.cos(angles), (1, 2 * heads))
    sines = jnp.tile(jnp.concatenate([-jnp.sin(angles), jnp.sin(angles)], 1), (1, heads))

    gain_one = gain_first.astype(FULL)[:, None]
    gain_two = gain_second.astype(FULL)[:, None]
    count = w_size - 1
    qkv_blocks = spread(qkv_weight, gain_one, plane, 3, 1, cols, pieces, [own_segments])

    tokens_all = lax.all_gather(own_tokens, PLANE, axis=0, tiled=True)
    out_received = from_others(out_weight, ACROSS) if pieces == across else []
    qkv_blocks, branch_pair, gate_up_own, *out_received = together(
        swap_group(qkv_blocks, PLANE),
        flip(cotangent[0], "p"),
        spread(gate_up_weight, gain_two, group, 2, w_size, units),
        *out_received,
    )
    if pieces == across:
        out_rows = jnp.zeros((across, *out_weight.shape), LOW)
        out_rows = put(out_rows, 0, [out_weight, *out_received], ACROSS).reshape(cols, width)
    else:
        out_rows = lax.all_gather(out_weight, EVERY, axis=0, tiled=True)
        out_rows = lax.dynamic_slice_in_dim(out_rows, lax.axis_index(PLANE) * cols, cols)
    qkv_own = qkv_blocks[:, : qkv_weight.shape[0]].reshape(-1, 3 * cols)
    all_segments = qkv_blocks[::4, qkv_weight.shape[0] :].reshape(2, -1)
    all_segments = all_segments.reshape(2, -1, 3, cols)[:, :, 0].reshape(2, -1)
    all_segments = all_segments[:, :length].astype(jnp.int32)
    branch_all = lax.all_gather(jnp.stack([cotangent[0], branch_pair]), PLANE)
    gate_up_own = swap_group(gate_up_own)
    weight_rows = group * gate_up_weight.shape[0]
    gate_up_own = gate_up_own.reshape(weight_rows, 2 * own_units)
    qkv_received = from_others(qkv_own, ACROSS)
    qkv_cols = jnp.zeros((across, *qkv_own.shape), LOW)
    qkv_cols = put(qkv_cols, 0, [qkv_own, *qkv_received], ACROSS).reshape(width, 3 * cols)
    ends = [0, weight_rows // 2, weight_rows]
    gate_up_parts = [gate_up_own[low:high] for low, high in zip(ends, ends[1:])]
    gate_up_cols = jnp.zeros((w_size, weight_rows, 2 * own_units), LOW)

    seg_col = all_segments.reshape(plane_rows, 1)
    seg_row = jnp.broadcast_to(all_segments[:, None], (2, 8, length)).reshape(16, length)
    scaled_ones, qkv_lows, logs, attended_heads, *out_parts = on_sequences(
        functools.partial(attend_kernel, heads),
        plane_wheres,
        [
            (tokens_all, length),
            (qkv_cols, 0),
            (out_rows, 0),
            (cosines, 0),
            (sines, 0),
            (seg_col, length),
            (seg_row, 8),
        ],
        [
            (((plane_rows, width), LOW), length),
            (((plane_rows, 3 * cols), LOW), length),
            (((plane_rows, cols), FULL), length),
            (((plane_rows, cols), LOW), length),
        ]
        + [(((2 * rows, width), LOW), -rows)] * 4,
        [pltpu.VMEM((length, width), FULL)],
        4 * length * width * 4 * cols + 8 * heads * length * length * LANES,
        2 * heads * length * length,
    )

    def norm_scale(values):
        return lax.rsqrt(jnp.mean(values * values, -1, keepdims=True) + EPSILON)

    def put_gate_up(whole, index, received):
        return put(whole, ends[index], [gate_up_parts[index], *received])

    moves = scatter_plane(out_parts)
    down_others = from_others(after(down_weight, *qkv_received))
    flips, _ = step(moves, next(moves))
    out_sum, (down_others, gate_up_parts) = step(moves, flips, [down_others, gate_up_parts])
    inputs = own_tokens.astype(FULL)
    residual = inputs + out_sum
    inverse_two = norm_scale(residual)
    scaled_two = residual * inverse_two
    scaled_twos = lax.all_gather(scaled_two.astype(LOW), GROUP, axis=0, tiled=True)
    received = down_others
    for index in range(2):
        received = from_others(after(gate_up_parts[index], *received))
        gate_up_cols = put_gate_up(gate_up_cols, index, received)
    gate_up_cols = gate_up_cols.reshape(width, 2 * own_units)
    down_rows = jnp.zeros((w_size, units, width), LOW)
    down_rows = put(down_rows, 0, [down_weight, *down_others]).reshape(own_units, width)

    unit_rows, gate_up_grads, *two_parts = on_sequences(
        feed_kernel,
        wheres,
        [(scaled_twos, length), (branch_all, cube_spec), (gate_up_cols, 0), (down_rows, 0)],
        [
            (((plane, 2, rows, own_units), LOW), unit_spec),
            (((group_rows, 2 * own_units), LOW), length),
        ]
        + [(((4 * rows, width), LOW), -rows)] * 4,
        [pltpu.VMEM((length, width), FULL)],
        40 * length * width * own_units,
        4 * length * own_units,
    )

    hiddens = unit_rows.reshape(group_rows, own_units)
    branch_rows = branch_all.reshape(group_rows, width)

    cuts = [0, weight_rows * 9 // 16, weight_rows]

    def gate_up_terms(left, index):
        return terms_for(left, gate_up_grads, cuts[index], cuts[index + 1])

    moves = scatter_steps(two_parts)
    down_terms = terms_for(hiddens, branch_rows, 0, units)
    late_scaled = after(scaled_twos, *down_terms)
    terms = [gate_up_terms(late_scaled, index) for index in range(2)]
    down_sent = [
        [term[: units // 2] for term in down_terms],
        [term[units // 2 :] for term in down_terms],
    ]
    flips, (terms, down_first) = step(moves, next(moves), [terms, to_others(down_sent[0])])
    mixed_term = product(after(hiddens, flips), down_rows).astype(LOW)
    down_second = to_others(after(down_sent[1], *down_first))
    flips, (down_second, mixed_term) = step(moves, flips, [down_second, mixed_term])
    down_received = [jnp.concatenate(parts, 0) for parts in zip(down_first, down_second)]
    mixed_sum = lax.psum_scatter(mixed_term, PLANE, scatter_dimension=0, tiled=True)
    weighted_two, _ = step(moves, flips)
    upstream = cotangent[0].astype(FULL)
    residual_grad = upstream + inverse_two * (
        weighted_two - scaled_two * jnp.mean(weighted_two * scaled_two, -1, keepdims=True)
    )
    attn_grad_low = residual_grad.astype(LOW)
    first_rows = to_others(after(terms[0], *down_second))
    late_scaled = after(scaled_twos, attn_grad_low)
    gate_up_own = rows_for(late_scaled, gate_up_grads, 0, 0, weight_rows)
    along_x, along_q, other, first_rows, gate_up_own = together(
        flip(attn_grad_low, "x"),
        flip(attn_grad_low, "q"),
        flip(attn_grad_low, "c"),
        first_rows,
        gate_up_own,
    )
    second_rows = to_others(after(terms[1], *first_rows))
    corner = flip(along_x, "q")
    blocks = [attn_grad_low, along_x, other, flip(along_x, "c")]
    held, out_sum = (), jnp.zeros((cols, width), FULL)
    for index in range(2):
        if index:
            along_q, corner = after((along_q, corner), out_sum)
            blocks = [along_q, corner, flip(along_q, "c"), flip(corner, "c")]
        *held, out_sum = on_sequences(
            functools.partial(attend_back_kernel, heads),
            jnp.concatenate([plane_wheres[index : index + 1], plane_wheres[2:]]),
            [(block, 0) for block in blocks]
            + [(qkv_lows, length), (logs, length), (attended_heads, length)]
            + [(array, 0) for array in (out_sum, qkv_cols, out_rows, cosines, sines)]
            + [(seg_col, length), (seg_row, 8)],
            [
                (((plane_rows, 3 * cols), LOW), length),
                (((plane_rows, width), LOW), length),
                (((cols, width), FULL), 0),
            ],
            [pltpu.VMEM((length, width), LOW)],
            2 * length * width * 5 * cols + 10 * heads * length * length * LANES,
            heads * length * length,
            held,
        )
    qkv_grads, one_term = held
    qkv_grads, one_term, out_sum, second_rows = together(
        qkv_grads, one_term, out_sum, second_rows
    )
    gate_up_received = [first_rows, second_rows]
    mixed_rows = after(mixed_sum, qkv_grads)
    mixed_sum = added(mixed_rows[:rows], [flip(mixed_rows[rows:], "p")])
    mixed = (residual + mixed_sum).astype(LOW)
    late_ones = after(scaled_ones, qkv_grads)
    qkv_terms = terms_for(late_ones, qkv_grads, 0, width // across, ACROSS)
    late_hiddens = after(hiddens, *qkv_terms)
    one_term = after(one_term, mixed_rows)
    weighted_one = lax.psum_scatter(one_term, PLANE, scatter_dimension=0, tiled=True)
    weighted_one = weighted_one.astype(FULL)
    rank = lax.axis_index(ACROSS)
    out_part = out_sum.reshape(across, cols // across, width)
    out_part, *out_terms = [
        lax.dynamic_index_in_dim(out_part, (rank - step) % across, 0, keepdims=False)
        for step in range(across)
    ]
    qkv_received = to_others(qkv_terms, ACROSS)
    gate_up_received = [jnp.concatenate(parts, 0) for parts in zip(*gate_up_received)]
    gate_up_mine = added(gate_up_own, gate_up_received)
    qkv_own = rows_for(late_ones, qkv_grads, 0, 0, width // across, ACROSS)
    down_own = rows_for(late_hiddens, branch_rows, 0, 0, units)
    gate_up_blocks = swap_group(gate_up_mine.astype(LOW).reshape(group, -1, 2 * own_units))
    qkv_mine = added(qkv_own, qkv_received).astype(LOW)
    down_grad = added(
        down_own, down_received
    )
    out_terms = after([term.astype(LOW) for term in out_terms], qkv_mine)
    out_grad = added(out_part, to_others(out_terms, ACROSS))
    if pieces != across:
        owners = [(z * plane + t, t * across + z) for z in range(across) for t in range(plane)]
        out_grad = lax.ppermute(out_grad.astype(LOW), EVERY, owners).astype(FULL)

    qkv_mine = after(qkv_mine.astype(LOW), gate_up_blocks)
    qkv_blocks = swap_group(qkv_mine.reshape(plane, -1, 3 * cols), PLANE)

    inverse_one = norm_scale(inputs)
    scaled_one = inputs * inverse_one
    input_grad = residual_grad + inverse_one * (
        weighted_one - scaled_one * jnp.mean(weighted_one * scaled_one, -1, keepdims=True)
    )
    gate_up_grad, gain_two_grad = collect(
        gate_up_blocks, gate_up_weight, gain_two, 2, w_size, units
    )
    qkv_grad, gain_one_grad = collect(qkv_blocks, qkv_weight, gain_one, 3, 1, cols, pieces)
    return (
        mixed[None],
        input_grad[None],
        gain_one_grad,
        qkv_grad,
        out_grad,
        gain_two_grad,
        gate_up_grad,
        down_grad,
    )


def solution(mesh):
    dp_size, _ = mesh.devices.shape
    fine = Mesh(mesh.devices.reshape(dp_size // 4, 2, 2, 2, 2), EVERY)
    token_spec = P(("w", "p", "q"), ("x", "c"), None)
    matrix, vector = P(EVERY, None), P(EVERY)
    return jax.shard_map(
        shards,
        mesh=fine,
        in_specs=(
            token_spec,
            P(("w", "p", "q"), None),
            vector,
            matrix,
            matrix,
            vector,
            matrix,
            matrix,
            token_spec,
        ),
        out_specs=(token_spec, token_spec, vector, matrix, matrix, vector, matrix, matrix),
        check_vma=False,
    )
```
